512 devices in a mesh: shift: 8 (over y, x_hi), dom: 32 (over x_lo, z), eh: 2 (over core).
Axes of the slice: x: 4 (x_hi: 2, x_lo: 2; x = x_hi * 2 + x_lo), y: 4, z: 16, core: 2. Of those that a mesh axis runs over, the one named last changes fastest.
Arguments:
- right_side: float32 [2, 512, 32, 128], P('eh', 'dom'), may hold values from -6 to 6
- shifts: float32 [8, 2], P('shift'), may hold values from 0.3 to 1.5
- quad_weights: float32 [8, 2], P('shift'), may hold values from -4 to 4
- hop_table: float32 [8, 2, 64, 64], replicated, may hold values from -0.3125 to 0.3125
- pair_table: float32 [4, 2, 64, 64], replicated, may hold values from -0.5 to 0.5
- hop_type: int32 [512, 3], P('dom'), may hold values from 0 to 7
- pair_type: int32 [512], P('dom'), may hold values from 0 to 3
Outputs:
- filtered: float32 [2, 512, 32, 128], P('eh', ('dom', 'shift'))
The draws below stay inside these ranges and needn't reach their ends.
All inputs are finite; a program needn't handle non-finite values.
Results may differ from the reference program's by a relative error of at most 0.0003.
Values sent between devices are 32-bit elements; how exact they have to be, the bound alone decides.
No kernel may reach another device: no remote copies, remote signals or barrier semaphores. Data moves between devices by JAX's collectives and lax.ppermute only.
A program may use at most 64 MiB of HBM per device.

```python
import jax
import jax.numpy as jnp
from jax import lax

ORB = 64
COLS = 32
ITERS = 2
TYPES = 8
PTYPES = 4
NBLK = 512
POINTS = 8


def draw_right_side(key, part):
    key = jax.random.fold_in(key, 11)
    key_entries, key_order = jax.random.split(key)
    order = jax.random.permutation(key_order, COLS)
    col_scale = jnp.exp(-4.605170186 * (order.astype(jnp.float32) + 0.5) / COLS)
    entries = jnp.clip(jax.random.normal(key_entries, (2, NBLK, COLS, 2 * ORB), jnp.float32), -6.0, 6.0)
    return entries * col_scale[None, None, :, None]


def with_ends(drawn, own_key, low, top_value):
    longest = drawn.shape.index(max(drawn.shape))
    spots = []
    for shift in (0, 1):
        where = [jax.random.randint(jax.random.fold_in(own_key, axis), (), 0, length) for axis, length in enumerate(drawn.shape)]
        where[longest] = (where[longest] + shift) % drawn.shape[longest]
        spots.append(tuple(where))
    return drawn.at[spots[0]].set(low).at[spots[1]].set(top_value)


def block_scale(stream_key, shape, pieces, smallest, top_value):
    def one(axis_at, parts):
        heights = jax.random.uniform(jax.random.fold_in(jax.random.fold_in(stream_key, 6), axis_at), (parts,), jnp.float32, smallest / len(pieces), top_value / len(pieces))
        return jnp.repeat(jnp.exp(heights), shape[axis_at] // parts).reshape((-1,) + (1,) * (len(shape) - axis_at - 1))

    factor_of = one(*pieces[0])
    for cut in pieces[1:]:
        factor_of = factor_of * one(*cut)
    return factor_of


def scatter_about(rng, extent, deviation, bound, cuts=(), dtype=jnp.bfloat16):
    drawn = jax.random.normal(rng, extent, jnp.float32) * deviation
    if len(cuts) > 0:
        drawn = block_scale(rng, extent, cuts, -0.22, 0.18) * drawn
    return jnp.clip(drawn, min=-bound, max=bound).astype(dtype)


def setup_inputs(seed: int = 0) -> dict:
    streams_of = jax.random.split(jax.random.key(seed), 8)
    return {
        "right_side": draw_right_side(jax.random.fold_in(streams_of[7], 71), 0),
        "shifts": jnp.clip(0.3 + 1.2 * jax.random.uniform(streams_of[1], (POINTS, 2), jnp.float32) ** block_scale(streams_of[1], (POINTS, 2), ((0, 8),), -0.2, 0.2), 0.3, 1.5),
        "quad_weights": scatter_about(streams_of[2], (POINTS, 2), 1.0, 4.0, ((0, 8),), jnp.float32),
        "hop_table": scatter_about(streams_of[3], (TYPES, 2, ORB, ORB), (6 * ORB) ** -0.5, 0.3125, (), jnp.float32),
        "pair_table": scatter_about(streams_of[4], (PTYPES, 2, ORB, ORB), (2 * ORB) ** -0.5, 0.5, (), jnp.float32),
        "hop_type": with_ends(jax.random.randint(streams_of[5], (NBLK, 3), 0, TYPES), jax.random.fold_in(streams_of[5], 1), 0, TYPES - 1).astype(jnp.int32),
        "pair_type": with_ends(jax.random.randint(streams_of[6], (NBLK,), 0, PTYPES), jax.random.fold_in(streams_of[6], 1), 0, PTYPES - 1).astype(jnp.int32),
    }


def flip(mats):
    return jnp.swapaxes(mats, -1, -2)


def real_form(real_part, imag_part):
    upper = jnp.concatenate([flip(real_part), flip(imag_part)], -1)
    lower = jnp.concatenate([-flip(imag_part), flip(real_part)], -1)
    return jnp.concatenate([upper, lower], -2)


def block_tables(hop_table, pair_table):
    hop_re, hop_im = hop_table[:, 0], hop_table[:, 1]
    pair_re, pair_im = pair_table[:, 0], pair_table[:, 1]
    sym_re = hop_re + flip(hop_re)
    sym_im = hop_im + flip(hop_im)
    onsite = jnp.stack([real_form(sym_re, sym_im), real_form(-sym_re, sym_im)])
    forward = jnp.stack([real_form(hop_re, hop_im), real_form(-hop_re, hop_im)])
    backward = jnp.stack([real_form(flip(hop_re), flip(hop_im)), real_form(-flip(hop_re), flip(hop_im))])
    pairing = jnp.stack([real_form(pair_re, pair_im), real_form(flip(pair_re), flip(pair_im))])
    return onsite, forward, backward, pairing


def block_mul(vec, mats):
    return jnp.einsum('bcj,bji->bci', vec, mats, precision=lax.Precision.HIGHEST)


def cscale(coef, vec):
    orb = vec.shape[-1] // 2
    coef_re = coef[0][None, None, :, None]
    coef_im = coef[1][None, None, :, None]
    vec_re, vec_im = vec[..., :orb], vec[..., orb:]
    return jnp.concatenate([coef_re * vec_re - coef_im * vec_im, coef_re * vec_im + coef_im * vec_re], -1)


def cmul(left, right):
    return jnp.stack([left[0] * right[0] - left[1] * right[1], left[0] * right[1] + left[1] * right[0]])


def cdiv(left, right):
    denom = jnp.maximum(right[0] * right[0] + right[1] * right[1], 1.0)
    return jnp.stack([(left[0] * right[0] + left[1] * right[1]) / denom, (left[1] * right[0] - left[0] * right[1]) / denom])


def bilinear(left, right):
    orb = left.shape[-1] // 2
    lre, lim = left[..., :orb], left[..., orb:]
    rre, rim = right[..., :orb], right[..., orb:]
    real_sum = jnp.sum(lre * rre - lim * rim, axis=(0, 1, 3))
    imag_sum = jnp.sum(lre * rim + lim * rre, axis=(0, 1, 3))
    return jnp.stack([real_sum, imag_sum])


def reference(right_side, shifts, quad_weights, hop_table, pair_table, hop_type, pair_type):
    onsite, forward, backward, pairing = block_tables(hop_table, pair_table)
    nblk = right_side.shape[1]
    cols = right_side.shape[2]
    types_pad = jnp.pad(hop_type, ((2, 2), (0, 0)))
    band_mats = []
    for side in range(2):
        band_mats.append((onsite[side][hop_type[:, 0]], forward[side][hop_type[:, 1]], forward[side][hop_type[:, 2]],
                          backward[side][types_pad[1:1 + nblk, 1]], backward[side][types_pad[0:nblk, 2]]))
    pair_mats = (pairing[0][pair_type], pairing[1][pair_type])

    def band(vec, mats):
        padded = jnp.pad(vec, ((2, 2), (0, 0), (0, 0)))
        total = block_mul(vec, mats[0])
        total = total + block_mul(padded[3:3 + nblk], mats[1]) + block_mul(padded[4:4 + nblk], mats[2])
        total = total + block_mul(padded[1:1 + nblk], mats[3]) + block_mul(padded[0:nblk], mats[4])
        return total

    def operate(vec, zval):
        elec = band(vec[0], band_mats[0]) + block_mul(vec[1], pair_mats[0])
        hole = band(vec[1], band_mats[1]) + block_mul(vec[0], pair_mats[1])
        return cscale(zval, vec) - jnp.stack([elec, hole])

    def point(total, inputs):
        zpair, wpair = inputs
        zval = jnp.broadcast_to(zpair[:, None], (2, cols))
        wval = jnp.broadcast_to(wpair[:, None], (2, cols))
        sol = jnp.zeros_like(right_side)
        resid = right_side
        direc = right_side
        rho = bilinear(resid, resid)
        for step in range(ITERS):
            image = operate(direc, zval)
            alpha = cdiv(rho, bilinear(direc, image))
            sol = sol + cscale(alpha, direc)
            if step + 1 < ITERS:
                resid = resid - cscale(alpha, image)
                rho_next = bilinear(resid, resid)
                direc = resid + cscale(cdiv(rho_next, rho), direc)
                rho = rho_next
        return total + cscale(wval, sol), None

    start = jnp.zeros(right_side.shape, jnp.float32)
    filtered, unused = lax.scan(point, start, (shifts, quad_weights))
    return filtered
```

```python
import jax
import jax.numpy as jnp
from jax import lax
from jax.experimental import pallas as pl
from jax.experimental.pallas import tpu as pltpu
from jax.sharding import PartitionSpec as P

ALL = ("shift", "dom", "eh")
F32 = jnp.float32
BF16 = jnp.bfloat16
SHIFTS, DOMS, EHS = 8, 32, 2
BLK, COLS, LANES = 16, 32, 128
HALF = BLK // 2
WIN = HALF + 6
REACH = HALF + 2
VM = pltpu.CompilerParams(vmem_limit_bytes=48 * 1024 * 1024)


def flat(s, d, e):
    return (s * DOMS + d) * EHS + e


def halo_pairs():
    pairs = []
    for s in range(SHIFTS):
        by = 1 if s < SHIFTS // 2 else -1
        for d in range(DOMS):
            if 0 <= d + by < DOMS:
                pairs += [(flat(s, d, e), flat(s, d + by, e)) for e in range(EHS)]
    return pairs


def moment_groups():
    groups = []
    for turn in range(2):
        for gx in range(2):
            for e in range(EHS):
                group = []
                for d in range(DOMS):
                    z, xl = d % 16, d // 16
                    ylo, yhi = ((1, 2), (0, 3))[turn ^ ((z % 8) // 4)]
                    xh = gx ^ xl
                    group += [flat(ylo * 2 + xh, d, e), flat(yhi * 2 + xh, d, e)]
                groups.append(group)
    return groups


POINT_ROWS = [2 * d + k for d in (0, 4, 16, 20) for k in range(2)]


def halves(shape):
    lane = lax.broadcasted_iota(jnp.int32, shape, len(shape) - 1)
    return jnp.where(lane < LANES // 2, 1.0, -1.0).astype(F32)


def split3(x):
    a = x.astype(BF16)
    r = x - a.astype(F32)
    b = r.astype(BF16)
    c = (r - b.astype(F32)).astype(BF16)
    return a, b, c


def quad(a, b, c, d):
    return jnp.concatenate(
        [jnp.concatenate([a, b], 1), jnp.concatenate([c, d], 1)], 0
    )


def tables_kernel(hop_ref, pair_ref, hop_out, pair_out):
    def put(out, at, mat):
        out[at] = jnp.concatenate(split3(mat), 1)

    for t in range(8):
        re, im = hop_ref[t, 0], hop_ref[t, 1]
        ret, imt = re.T, im.T
        bwd = quad(re, im, -im, re)
        fwd = quad(ret, imt, -imt, ret)
        put(hop_out, 3 * t, fwd)
        put(hop_out, 3 * t + 1, bwd)
        put(hop_out, 3 * t + 2, fwd + bwd)
    for t in range(4):
        re, im = pair_ref[t, 0], pair_ref[t, 1]
        ret, imt = re.T, im.T
        put(pair_out, 2 * t, quad(ret, imt, imt, -ret))
        put(pair_out, 2 * t + 1, quad(-re, im, im, re))


def product(lhs, tabs):
    rows = lhs.shape[0] // 3
    both = jnp.concatenate([t[:, : 2 * LANES] for t in tabs], 0)
    third = jnp.concatenate([t[:, 2 * LANES :] for t in tabs], 0)
    big = jnp.dot(lhs, both, preferred_element_type=F32)
    small = jnp.dot(lhs[:rows], third, preferred_element_type=F32)
    small = small + big[2 * rows :, :LANES] + big[rows : 2 * rows, LANES:]
    small = small + (big[:rows, LANES:] + big[rows : 2 * rows, :LANES])
    return big[:rows, :LANES] + small


def moments_kernel(
    hop_s, pair_s, shift_s, weight_s, both_ref, recv_ref, hop_t, pair_t,
    mom_ref, img_ref, u_ref, us_ref, g_ref, gs_ref, rt_ref, wt_ref, sem,
):
    point, eh = lax.axis_index("shift"), lax.axis_index("eh")
    low = point < SHIFTS // 2
    base = jnp.where(low, 0, HALF)
    types = pltpu.make_async_copy(recv_ref.at[pl.ds(256, 8)], rt_ref, sem)
    types.start()
    sign = halves((1, LANES))

    def load(at, elec, hole):
        u_ref[at, :COLS] = elec
        u_ref[at, COLS:] = hole * sign

    @pl.when(low)
    def _():
        for j in range(2):
            load(j, recv_ref[pl.ds((2 + j) * COLS, COLS)], recv_ref[pl.ds((6 + j) * COLS, COLS)])
        for j in range(12):
            load(2 + j, both_ref[0, j], both_ref[1, j])

    @pl.when(jnp.logical_not(low))
    def _():
        for j in range(10):
            load(j, both_ref[0, 6 + j], both_ref[1, 6 + j])
        for j in range(4):
            load(10 + j, recv_ref[pl.ds(j * COLS, COLS)], recv_ref[pl.ds((4 + j) * COLS, COLS)])

    for j in range(WIN):
        us_ref[j] = jnp.concatenate(split3(u_ref[j]), 0)
    types.wait()
    valid = rt_ref[0, 64]
    for j in range(WIN):
        i = base + (j - 2)
        own = jnp.logical_and(i >= 0, i < BLK)
        at = jnp.bitwise_and(i, BLK - 1)
        for c in range(4):
            here = hop_s[at, c] if c < 3 else pair_s[at]
            there = rt_ref[0, at * 4 + c].astype(jnp.int32)
            wt_ref[j, c] = jnp.where(own, here, there)

    def hop(kind, j, c):
        return hop_t[3 * wt_ref[j, c] + kind]

    def crossed(ref, at, sgn=None):
        zero = jnp.zeros((COLS, LANES), BF16)
        rows = []
        for part in range(3):
            x = ref[at, pl.ds(part * 2 * COLS + COLS, COLS)]
            rows += [x if sgn is None else -x, zero]
        return jnp.concatenate(rows, 0)

    def crossed_up(ref, at):
        zero = jnp.zeros((COLS, LANES), BF16)
        rows = []
        for part in range(3):
            rows += [zero, ref[at, pl.ds(part * 2 * COLS, COLS)]]
        return jnp.concatenate(rows, 0)

    for m in range(REACH):
        j = m + 2
        lhs = jnp.concatenate(
            [us_ref[m + k] for k in range(5)] + [crossed(us_ref, j), crossed_up(us_ref, j)], 1
        )
        tabs = [
            hop(1, j - 2, 2),
            hop(1, j - 1, 1),
            hop(2, j, 0),
            hop(0, j, 1),
            hop(0, j, 2),
            pair_t[2 * wt_ref[j, 3]],
            pair_t[2 * wt_ref[j, 3] + 1],
        ]
        img = product(lhs, tabs)
        if m >= HALF:
            img = jnp.where(jnp.logical_or(low, valid > 0.5), img, 0.0)
        g_ref[m] = img
        gs_ref[m] = jnp.concatenate(split3(img), 0)

    zero = jnp.zeros((2 * COLS, LANES), F32)
    re = [zero] * 4
    im = [zero] * 4
    for m in range(HALF):
        j = m + 2
        lhs = jnp.concatenate([gs_ref[m + k] for k in range(3)] + [crossed(gs_ref, m, -1)], 1)
        tabs = [hop(0, j, 0), hop(0, j, 1), hop(0, j, 2), pair_t[2 * wt_ref[j, 3]]]
        y = product(lhs, tabs)
        u, g = u_ref[j], g_ref[m]
        gr = pltpu.roll(g, LANES // 2, 1)
        for n, (a, b, br) in enumerate(
            ((u, u, pltpu.roll(u, LANES // 2, 1)), (u, g, gr), (g, g, gr), (g, y, pltpu.roll(y, LANES // 2, 1)))
        ):
            re[n] = re[n] + a * b
            im[n] = im[n] + a * br
    ones = jnp.ones((8, LANES), F32)
    rows = []
    for n in range(4):
        s = 1.0 if n in (0, 2) else -1.0
        w = 2.0 if n == 3 else 1.0
        rows.append(w * sign * (re[n][:COLS] + s * re[n][COLS:]))
        rows.append(w * (im[n][:COLS] - s * im[n][COLS:]))
    sums = [
        lax.dot_general(
            ones, jnp.concatenate(rows[4 * k : 4 * k + 4], 0), (((1,), (1,)), ((), ())),
            precision=lax.Precision.HIGHEST, preferred_element_type=F32,
        )
        for k in range(2)
    ]
    lane = lax.broadcasted_iota(jnp.int32, (1, LANES), 1)
    par = jnp.where(lane == 0, shift_s[0, 0], jnp.where(lane == 1, shift_s[0, 1], 0.0))
    par = jnp.where(lane == 2, weight_s[0, 0], jnp.where(lane == 3, weight_s[0, 1], par))
    mine = jnp.concatenate([sums[0][:1], sums[1][:1], par, jnp.zeros_like(par)], 0)
    mom_ref[...] = jnp.broadcast_to(mine[None], mom_ref.shape)
    first = 2 * jnp.bitwise_and(point, 3)
    turn = jnp.where(eh == 0, jnp.ones_like(sign), -sign)
    for k in range(2):
        img_ref[k] = turn * g_ref[first + k, pl.ds(pl.multiple_of(eh * COLS, COLS), COLS)]


def cmul(a, b):
    return a[0] * b[0] - a[1] * b[1], a[0] * b[1] + a[1] * b[0]


def cadd(a, b):
    return a[0] + b[0], a[1] + b[1]


def cdiv(a, b):
    denom = jnp.maximum(b[0] * b[0] + b[1] * b[1], 1.0)
    return (a[0] * b[0] + a[1] * b[1]) / denom, (a[1] * b[0] - a[0] * b[1]) / denom


def combine_kernel(mom_ref, right_ref, img_ref, out_ref):
    total = jnp.sum(mom_ref[...], axis=0)
    pts = jnp.concatenate([mom_ref[j, 2:3] for j in POINT_ROWS], 0)

    def moment(n):
        row = total[n // 2 : n // 2 + 1]
        at = (n % 2) * 64
        return tuple(
            jnp.broadcast_to(row[:, at + k * COLS : at + (k + 1) * COLS], (SHIFTS, COLS))
            for k in range(2)
        )

    def param(n):
        return tuple(
            jnp.broadcast_to(pts[:, n + k : n + k + 1], (SHIFTS, COLS)) for k in range(2)
        )

    m0, m1, m2, m3 = (moment(n) for n in range(4))
    z, w = param(0), param(2)

    def minus(a, b):
        return a[0] - b[0], a[1] - b[1]

    def twice(a):
        return 2.0 * a[0], 2.0 * a[1]

    a0 = cdiv(m0, minus(cmul(z, m0), m1))
    az = cmul(a0, z)
    s = (1.0 - az[0], -az[1])
    s2, sa, aa = cmul(s, s), cmul(s, a0), cmul(a0, a0)
    rho = cadd(cadd(cmul(s2, m0), twice(cmul(sa, m1))), cmul(aa, m2))
    c = cadd(s, cdiv(rho, m0))
    cc, ca = cmul(c, c), cmul(c, a0)
    pp = cadd(cadd(cmul(cc, m0), twice(cmul(ca, m1))), cmul(aa, m2))
    php = cadd(cadd(cmul(cc, m1), twice(cmul(ca, m2))), cmul(aa, m3))
    a1 = cdiv(rho, minus(cmul(z, pp), php))
    c0 = cmul(w, cadd(a0, cmul(a1, c)))
    c1 = cmul(w, cmul(a1, a0))
    rows = [jnp.sum(x, axis=0, keepdims=True) for x in (*c0, *c1)]
    stack = jnp.concatenate(rows + [jnp.zeros((4, COLS), F32)], 0)
    stack = jnp.concatenate([stack, jnp.zeros((8, LANES - COLS), F32)], 1)
    cols = stack.T[:COLS]
    sign = -halves((1, LANES))
    point = lax.axis_index("shift")
    for k in range(2):
        b, g = right_ref[0, 2 * point + k], img_ref[k]
        out = cols[:, 0:1] * b + cols[:, 1:2] * (pltpu.roll(b, LANES // 2, 1) * sign)
        out = out + cols[:, 2:3] * g + cols[:, 3:4] * (pltpu.roll(g, LANES // 2, 1) * sign)
        out_ref[0, k] = out


def body(right_side, shifts, quad_weights, hop_table, pair_table, hop_type, pair_type):
    smem = pl.BlockSpec(memory_space=pltpu.SMEM)
    vmem = pl.BlockSpec(memory_space=pltpu.VMEM)
    low = lax.axis_index("shift") < SHIFTS // 2
    types = jnp.concatenate([hop_type, pair_type[:, None]], 1).astype(F32).reshape(1, 64)
    types = jnp.concatenate([types, jnp.ones((1, 64), F32)], 1)
    both = lax.all_gather(right_side[0], "eh")
    edge = lax.dynamic_slice_in_dim(both, jnp.where(low, BLK - 4, 0), 4, 1)
    payload = jnp.concatenate(
        [edge.reshape(8 * COLS, LANES), jnp.broadcast_to(types, (8, LANES))], 0
    )
    recv = lax.ppermute(payload, ALL, halo_pairs())
    hop_t, pair_t = pl.pallas_call(
        tables_kernel,
        out_shape=[
            jax.ShapeDtypeStruct((24, LANES, 3 * LANES), BF16),
            jax.ShapeDtypeStruct((8, LANES, 3 * LANES), BF16),
        ],
        in_specs=[vmem, vmem],
        out_specs=[vmem, vmem],
        compiler_params=VM,
        name="tables",
    )(hop_table, pair_table)
    mom, img = pl.pallas_call(
        moments_kernel,
        out_shape=[
            jax.ShapeDtypeStruct((2 * DOMS, 4, LANES), F32),
            jax.ShapeDtypeStruct((2, COLS, LANES), F32),
        ],
        in_specs=[smem] * 4 + [vmem] * 4,
        out_specs=[vmem, vmem],
        scratch_shapes=[
            pltpu.VMEM((WIN, 2 * COLS, LANES), F32),
            pltpu.VMEM((WIN, 6 * COLS, LANES), BF16),
            pltpu.VMEM((REACH, 2 * COLS, LANES), F32),
            pltpu.VMEM((REACH, 6 * COLS, LANES), BF16),
            pltpu.SMEM((8, LANES), F32),
            pltpu.SMEM((WIN, 4), jnp.int32),
            pltpu.SemaphoreType.DMA,
        ],
        compiler_params=VM,
        name="moments",
    )(hop_type, pair_type, shifts, quad_weights, both, recv, hop_t, pair_t)
    parts = lax.all_to_all(mom, ALL, 0, 0, axis_index_groups=moment_groups())
    return pl.pallas_call(
        combine_kernel,
        out_shape=jax.ShapeDtypeStruct((1, 2, COLS, LANES), F32),
        in_specs=[vmem, vmem, vmem],
        out_specs=vmem,
        compiler_params=VM,
        name="combine",
    )(parts, right_side, img)


def solution(mesh):
    placed = (
        P("eh", "dom", None, None),
        P("shift", None),
        P("shift", None),
        P(),
        P(),
        P("dom", None),
        P("dom"),
    )
    return jax.shard_map(
        body,
        mesh=mesh,
        in_specs=placed,
        out_specs=P("eh", ("dom", "shift"), None, None),
        check_vma=False,
    )
```

```python
import jax
import jax.numpy as jnp
from jax import lax
from jax.experimental import pallas as pl
from jax.experimental.pallas import tpu as pltpu
from jax.sharding import PartitionSpec as P

ALL = ("shift", "dom", "eh")
F32 = jnp.float32
BF16 = jnp.bfloat16
SHIFTS, DOMS, EHS = 8, 32, 2
BLK, COLS, LANES = 16, 32, 128
HALF = BLK // 2
WIN = HALF + 6
REACH = HALF + 2
VM = pltpu.CompilerParams(vmem_limit_bytes=24 * 1024 * 1024)


def flat(s, d, e):
    return (s * DOMS + d) * EHS + e


TURNS = {(0, 1): 1, (1, 0): 2, (1, 1): 3, (2, 0): 4, (16, 1): 5, (17, 0): 6, (17, 1): 7}
POINT_AT = [(0, 0)] + list(TURNS)


def halo_pairs():
    pairs = []
    for s in range(SHIFTS):
        for d in range(DOMS):
            for e in range(EHS):
                source = d - 1 + 2 * e
                if 0 <= source < DOMS:
                    turn = TURNS.get((d, e), 0)
                    pairs.append((flat(s ^ turn, source, e), flat(s, d, e)))
    return pairs


def halves(shape):
    lane = lax.broadcasted_iota(jnp.int32, shape, len(shape) - 1)
    return jnp.where(lane < LANES // 2, 1.0, -1.0).astype(F32)


def split3(x):
    a = x.astype(BF16)
    r = x - a.astype(F32)
    b = r.astype(BF16)
    c = (r - b.astype(F32)).astype(BF16)
    return a, b, c


def quad(a, b, c, d):
    return jnp.concatenate(
        [jnp.concatenate([a, b], 1), jnp.concatenate([c, d], 1)], 0
    )


def tables_kernel(hop_ref, pair_ref, hop_out, pair_out):
    def put(out, at, mat):
        out[at] = jnp.concatenate(split3(mat), 1)

    for t in range(8):
        re, im = hop_ref[t, 0], hop_ref[t, 1]
        ret, imt = re.T, im.T
        bwd = quad(re, im, -im, re)
        fwd = quad(ret, imt, -imt, ret)
        put(hop_out, 3 * t, fwd)
        put(hop_out, 3 * t + 1, bwd)
        put(hop_out, 3 * t + 2, fwd + bwd)
    for t in range(4):
        re, im = pair_ref[t, 0], pair_ref[t, 1]
        ret, imt = re.T, im.T
        put(pair_out, 2 * t, quad(ret, imt, imt, -ret))
        put(pair_out, 2 * t + 1, quad(-re, im, im, re))


def product(lhs, tabs):
    rows = lhs.shape[0] // 3
    both = jnp.concatenate([t[:, : 2 * LANES] for t in tabs], 0)
    third = jnp.concatenate([t[:, 2 * LANES :] for t in tabs], 0)
    big = jnp.dot(lhs, both, preferred_element_type=F32)
    small = jnp.dot(lhs[:rows], third, preferred_element_type=F32)
    small = small + big[2 * rows :, :LANES] + big[rows : 2 * rows, LANES:]
    small = small + (big[:rows, LANES:] + big[rows : 2 * rows, :LANES])
    return big[:rows, :LANES] + small


def crossed(block):
    ref, at = block
    zero = jnp.zeros((COLS, LANES), BF16)
    rows = []
    for part in range(3):
        rows += [ref[at, pl.ds((2 * part + 1) * COLS, COLS)], zero]
    return jnp.concatenate(rows, 0)


def crossed_up(block):
    ref, at = block
    zero = jnp.zeros((COLS, LANES), BF16)
    rows = []
    for part in range(3):
        rows += [zero, ref[at, pl.ds(2 * part * COLS, COLS)]]
    return jnp.concatenate(rows, 0)


def image(blocks, hop_t, pair_t, kinds):
    back2, back1, here, on1, on2, pair = kinds
    lhs = [ref[at] for ref, at in blocks]
    lhs += [crossed(blocks[2]), crossed_up(blocks[2])]
    tabs = [hop_t[3 * back2 + 1], hop_t[3 * back1 + 1], hop_t[3 * here + 2]]
    tabs += [hop_t[3 * on1], hop_t[3 * on2], pair_t[2 * pair], pair_t[2 * pair + 1]]
    return product(jnp.concatenate(lhs, 1), tabs)


def forward_image(blocks, hop_t, pair_t, kinds):
    here, on1, on2, pair = kinds
    lhs = [ref[at] for ref, at in blocks] + [-crossed(blocks[0])]
    tabs = [hop_t[3 * here], hop_t[3 * on1], hop_t[3 * on2], pair_t[2 * pair]]
    return product(jnp.concatenate(lhs, 1), tabs)


def swap(x):
    return pltpu.roll(x, LANES // 2, 1)


def add_pairs(re, im, n, a, b, b_swapped):
    re[n] = a * b if re[n] is None else re[n] + a * b
    im[n] = a * b_swapped if im[n] is None else im[n] + a * b_swapped


def fetch_kernel(
    hop_s, pair_s, shift_ref, weight_ref, hop_ref, pair_ref,
    facts_ref, hop_v, pair_v,
    hop_k, pair_k, shift_v, weight_v, sem,
):
    copies = [
        pltpu.make_async_copy(source, to, sem.at[n])
        for n, (source, to) in enumerate(
            (
                (hop_s, hop_k),
                (pair_s, pair_k),
                (shift_ref, shift_v),
                (weight_ref, weight_v),
                (hop_ref, hop_v),
                (pair_ref, pair_v),
            )
        )
    ]
    for c in copies:
        c.start()
    facts_ref[...] = jnp.zeros_like(facts_ref)
    facts_ref[6:7] = jnp.ones((1, LANES), F32)
    for c in copies:
        c.wait()
    facts_ref[0:3, :BLK] = hop_k[...].astype(F32)
    facts_ref[3:4, :BLK] = pair_k[...].astype(F32)
    facts_ref[4:5, :2] = shift_v[...]
    facts_ref[5:6, :2] = weight_v[...]


def parts_of(elec, hole, sign):
    return jnp.concatenate(split3(jnp.concatenate([elec, hole * sign], 0)), 0)


def inner_kernel(
    win_ref, own_ref, hop_t, pair_t,
    us_ref, g_ref, gs_ref, acc_ref,
    own_s, kind_s, sem,
):
    facts = pltpu.make_async_copy(own_ref.at[pl.ds(8 * COLS, 8)], own_s, sem)
    facts.start()
    low = lax.axis_index("eh") == 0
    sign = halves((1, LANES))
    for a in range(10):
        us_ref[a] = parts_of(win_ref[0, a], win_ref[1, a], sign)
    facts.wait()
    for a in range(8):
        for c in range(4):
            kind_s[a, c] = jnp.where(low, own_s[c, a], own_s[c, 6 + a]).astype(jnp.int32)
    re, im = [None] * 4, [None] * 4
    for k in range(6):
        kinds = [kind_s[k, 2], kind_s[k + 1, 1]] + [kind_s[k + 2, c] for c in range(4)]
        g = image([(us_ref, k + n) for n in range(5)], hop_t, pair_t, kinds)
        g_ref[k] = g
        gs_ref[k] = jnp.concatenate(split3(g), 0)
        u = jnp.concatenate([win_ref[0, k + 2], win_ref[1, k + 2] * sign], 0)
        add_pairs(re, im, 0, u, u, swap(u))
        add_pairs(re, im, 1, u, g, swap(g))
        add_pairs(re, im, 2, g, g, swap(g))
    for k in range(4):
        kinds = [kind_s[k + 2, c] for c in range(4)]
        y = forward_image([(gs_ref, k + n) for n in range(3)], hop_t, pair_t, kinds)
        add_pairs(re, im, 3, g_ref[k], y, swap(y))
    for n in range(4):
        acc_ref[2 * n] = re[n]
        acc_ref[2 * n + 1] = im[n]


def outer_side(
    low, win_ref, both_ref, recv_ref, hop_t, pair_t, us_in, g_in, gs_in, acc_ref,
    total_ref, us_new, g_ref, gs_new, own_s, recv_s, kind_s, waits, valid,
):
    off = 2 if low else 0
    base = 0 if low else HALF
    sign = halves((1, LANES))
    edge = [0, 1, 12, 13] if low else [10, 11, 12, 13]
    for n, j in enumerate(edge):
        i = base + j - 2
        if 0 <= i < BLK:
            elec, hole = both_ref[0, i], both_ref[1, i]
        else:
            at = i % 4
            elec = recv_ref[pl.ds(at * COLS, COLS)]
            hole = recv_ref[pl.ds((4 + at) * COLS, COLS)]
        us_new[n] = parts_of(elec, hole, sign)
    for k in range(6):
        g_ref[off + k] = g_in[k]
    for c in waits:
        c.wait()
    for j in range(WIN - 2):
        i = base + j - 2
        for c in range(4):
            fact = own_s[c, i] if 0 <= i < BLK else recv_s[c, i % BLK]
            kind_s[j, c] = fact.astype(jnp.int32)

    def us(j):
        return (us_new, edge.index(j)) if j in edge else (us_in, j - off)

    images = [0, 1, 8, 9] if low else [6, 7, 8, 9]

    def gs(m):
        return (gs_new, images.index(m)) if m in images else (gs_in, m - off)

    re = [acc_ref[2 * n] for n in range(4)]
    im = [acc_ref[2 * n + 1] for n in range(4)]
    for n, m in enumerate(images):
        j = m + 2
        kinds = [kind_s[j - 2, 2], kind_s[j - 1, 1]] + [kind_s[j, c] for c in range(4)]
        g = image([us(j - 2 + k) for k in range(5)], hop_t, pair_t, kinds)
        if base + m >= BLK:
            g = jnp.where(valid(), g, 0.0)
        g_ref[m] = g
        gs_new[n] = jnp.concatenate(split3(g), 0)
        if m < HALF:
            i = base + m
            u = jnp.concatenate([both_ref[0, i], both_ref[1, i] * sign], 0)
            add_pairs(re, im, 0, u, u, swap(u))
            add_pairs(re, im, 1, u, g, swap(g))
            add_pairs(re, im, 2, g, g, swap(g))
    for m in [0, 1, 6, 7] if low else [4, 5, 6, 7]:
        kinds = [kind_s[m + 2, c] for c in range(4)]
        y = forward_image([gs(m + k) for k in range(3)], hop_t, pair_t, kinds)
        add_pairs(re, im, 3, g_ref[m], y, swap(y))
    for n in range(4):
        s = 1.0 if n in (0, 2) else -1.0
        w = 2.0 if n == 3 else 1.0
        total_ref[2 * n] = w * sign * (re[n][:COLS] + s * re[n][COLS:])
        total_ref[2 * n + 1] = w * (im[n][:COLS] - s * im[n][COLS:])


def outer_kernel(
    win_ref, both_ref, own_ref, recv_ref, hop_t, pair_t, us_in, g_in, gs_in, acc_ref,
    send_ref, img_ref,
    total_ref, us_new, g_ref, gs_new, own_s, recv_s, kind_s, sem,
):
    copies = [
        pltpu.make_async_copy(own_ref.at[pl.ds(8 * COLS, 8)], own_s, sem.at[0]),
        pltpu.make_async_copy(recv_ref.at[pl.ds(8 * COLS, 8)], recv_s, sem.at[1]),
    ]
    for c in copies:
        c.start()
    point, eh = lax.axis_index("shift"), lax.axis_index("eh")

    def valid():
        return recv_s[6, 0] > 0.5

    for side in range(2):

        @pl.when(eh == side)
        def _(side=side):
            outer_side(
                side == 0, win_ref, both_ref, recv_ref, hop_t, pair_t, us_in, g_in, gs_in, acc_ref,
                total_ref, us_new, g_ref, gs_new, own_s, recv_s, kind_s, copies, valid,
            )

    low = eh == 0
    sign = halves((1, LANES))
    ones = jnp.ones((8, LANES), F32)
    for k in range(2):
        total = lax.dot_general(
            ones, total_ref[4 * k : 4 * k + 4].reshape(4 * COLS, LANES), (((1,), (1,)), ((), ())),
            precision=lax.Precision.HIGHEST, preferred_element_type=F32,
        )
        send_ref[k : k + 1] = total[:1]
    facts = jnp.where(valid(), recv_ref[8 * COLS :], own_ref[8 * COLS :])
    send_ref[2:3] = facts[4:5] + pltpu.roll(facts[5:6], 2, 1)
    send_ref[3:8] = jnp.zeros((5, LANES), F32)
    first = 2 * jnp.bitwise_and(point, 3)
    for k in range(2):
        g = g_ref[first + k]
        elec, hole = g[:COLS], -sign * g[COLS:]
        img_ref[k] = jnp.where(low, elec, hole)
        send_ref[(1 + 4 * k) * 8 : (5 + 4 * k) * 8] = jnp.where(low, hole, elec)


def cmul(a, b):
    return a[0] * b[0] - a[1] * b[1], a[0] * b[1] + a[1] * b[0]


def cadd(a, b):
    return a[0] + b[0], a[1] + b[1]


def cdiv(a, b):
    denom = jnp.maximum(b[0] * b[0] + b[1] * b[1], 1.0)
    return (a[0] * b[0] + a[1] * b[1]) / denom, (a[1] * b[0] - a[0] * b[1]) / denom


def combine_kernel(mom_ref, right_ref, img_ref, sent_ref, out_ref):
    total = jnp.sum(mom_ref[...], axis=0)
    pts = jnp.concatenate([mom_ref[d, 2 + e : 3 + e] for d, e in POINT_AT], 0)

    def moment(n):
        row = total[n // 2 : n // 2 + 1]
        at = (n % 2) * 64
        return tuple(
            jnp.broadcast_to(row[:, at + k * COLS : at + (k + 1) * COLS], (SHIFTS, COLS))
            for k in range(2)
        )

    def param(n):
        return tuple(
            jnp.broadcast_to(pts[:, n + k : n + k + 1], (SHIFTS, COLS)) for k in range(2)
        )

    m0, m1, m2, m3 = (moment(n) for n in range(4))
    z, w = param(0), param(2)

    def minus(a, b):
        return a[0] - b[0], a[1] - b[1]

    def twice(a):
        return 2.0 * a[0], 2.0 * a[1]

    a0 = cdiv(m0, minus(cmul(z, m0), m1))
    az = cmul(a0, z)
    s = (1.0 - az[0], -az[1])
    s2, sa, aa = cmul(s, s), cmul(s, a0), cmul(a0, a0)
    rho = cadd(cadd(cmul(s2, m0), twice(cmul(sa, m1))), cmul(aa, m2))
    c = cadd(s, cdiv(rho, m0))
    cc, ca = cmul(c, c), cmul(c, a0)
    pp = cadd(cadd(cmul(cc, m0), twice(cmul(ca, m1))), cmul(aa, m2))
    php = cadd(cadd(cmul(cc, m1), twice(cmul(ca, m2))), cmul(aa, m3))
    a1 = cdiv(rho, minus(cmul(z, pp), php))
    c0 = cmul(w, cadd(a0, cmul(a1, c)))
    c1 = cmul(w, cmul(a1, a0))
    rows = [jnp.sum(x, axis=0, keepdims=True) for x in (*c0, *c1)]
    stack = jnp.concatenate(rows + [jnp.zeros((4, COLS), F32)], 0)
    stack = jnp.concatenate([stack, jnp.zeros((8, LANES - COLS), F32)], 1)
    cols = stack.T[:COLS]
    sign = -halves((1, LANES))
    point = lax.axis_index("shift")
    holder = (point >= SHIFTS // 2).astype(jnp.int32)
    mine = lax.axis_index("eh") == holder
    for k in range(2):
        b = right_ref[0, 2 * point + k]
        g = jnp.where(mine, img_ref[k], sent_ref[holder, (1 + 4 * k) * 8 : (5 + 4 * k) * 8])
        out = cols[:, 0:1] * b + cols[:, 1:2] * (pltpu.roll(b, LANES // 2, 1) * sign)
        out = out + cols[:, 2:3] * g + cols[:, 3:4] * (pltpu.roll(g, LANES // 2, 1) * sign)
        out_ref[0, k] = out


def body(right_side, shifts, quad_weights, hop_table, pair_table, hop_type, pair_type):
    vmem = pl.BlockSpec(memory_space=pltpu.VMEM)
    low = lax.axis_index("eh") == 0
    inputs = (hop_type.T, pair_type[None], shifts, quad_weights, hop_table, pair_table)
    facts, hops, pairs = pl.pallas_call(
        fetch_kernel,
        out_shape=[
            jax.ShapeDtypeStruct((8, LANES), F32),
            jax.ShapeDtypeStruct(hop_table.shape, F32),
            jax.ShapeDtypeStruct(pair_table.shape, F32),
        ],
        in_specs=[pl.BlockSpec(memory_space=pltpu.HBM)] * 6,
        out_specs=[vmem] * 3,
        scratch_shapes=[
            pltpu.VMEM((3, BLK), jnp.int32),
            pltpu.VMEM((1, BLK), jnp.int32),
            pltpu.VMEM((1, 2), F32),
            pltpu.VMEM((1, 2), F32),
            pltpu.SemaphoreType.DMA((6,)),
        ],
        compiler_params=VM,
        name="fetch",
    )(*(pltpu.with_memory_space_constraint(x, pltpu.HBM) for x in inputs))
    both = lax.all_gather(right_side[0], "eh")
    edge = lax.dynamic_slice_in_dim(both, jnp.where(low, BLK - 4, 0), 4, 1)
    own = jnp.concatenate([edge.reshape(8 * COLS, LANES), facts], 0)
    recv = lax.ppermute(own, ALL, halo_pairs())
    hop_t, pair_t = pl.pallas_call(
        tables_kernel,
        out_shape=[
            jax.ShapeDtypeStruct((24, LANES, 3 * LANES), BF16),
            jax.ShapeDtypeStruct((8, LANES, 3 * LANES), BF16),
        ],
        in_specs=[vmem] * 2,
        out_specs=[vmem] * 2,
        compiler_params=VM,
        name="tables",
    )(hops, pairs)
    win = lax.dynamic_slice_in_dim(both, jnp.where(low, 0, 6), 10, 1)
    us, g, gs, acc = pl.pallas_call(
        inner_kernel,
        out_shape=[
            jax.ShapeDtypeStruct((10, 6 * COLS, LANES), BF16),
            jax.ShapeDtypeStruct((6, 2 * COLS, LANES), F32),
            jax.ShapeDtypeStruct((6, 6 * COLS, LANES), BF16),
            jax.ShapeDtypeStruct((8, 2 * COLS, LANES), F32),
        ],
        in_specs=[vmem] * 4,
        out_specs=[vmem] * 4,
        scratch_shapes=[
            pltpu.SMEM((8, LANES), F32),
            pltpu.SMEM((8, 4), jnp.int32),
            pltpu.SemaphoreType.DMA,
        ],
        compiler_params=VM,
        name="inner",
    )(win, own, hop_t, pair_t)
    send, img = pl.pallas_call(
        outer_kernel,
        out_shape=[
            jax.ShapeDtypeStruct((72, LANES), F32),
            jax.ShapeDtypeStruct((2, COLS, LANES), F32),
        ],
        in_specs=[vmem] * 10,
        out_specs=[vmem] * 2,
        scratch_shapes=[
            pltpu.VMEM((8, COLS, LANES), F32),
            pltpu.VMEM((4, 6 * COLS, LANES), BF16),
            pltpu.VMEM((REACH, 2 * COLS, LANES), F32),
            pltpu.VMEM((4, 6 * COLS, LANES), BF16),
            pltpu.SMEM((8, LANES), F32),
            pltpu.SMEM((8, LANES), F32),
            pltpu.SMEM((WIN, 4), jnp.int32),
            pltpu.SemaphoreType.DMA((2,)),
        ],
        compiler_params=VM,
        name="outer",
    )(win, both, own, recv, hop_t, pair_t, us, g, gs, acc)
    sent = lax.all_gather(send, "eh")
    mom = jnp.concatenate([sent[0, :2] + sent[1, :2], sent[:, 2]], 0)
    mom = jnp.broadcast_to(mom[None], (DOMS, 4, LANES))
    parts = lax.all_to_all(mom, "dom", 0, 0)
    return pl.pallas_call(
        combine_kernel,
        out_shape=jax.ShapeDtypeStruct((1, 2, COLS, LANES), F32),
        in_specs=[vmem] * 4,
        out_specs=vmem,
        compiler_params=VM,
        name="combine",
    )(parts, right_side, img, sent)


def solution(mesh):
    placed = (
        P("eh", "dom", None, None),
        P("shift", None),
        P("shift", None),
        P(),
        P(),
        P("dom", None),
        P("dom"),
    )
    return jax.shard_map(
        body,
        mesh=mesh,
        in_specs=placed,
        out_specs=P("eh", ("dom", "shift"), None, None),
        check_vma=False,
    )
```

```python
import jax
import jax.numpy as jnp
from jax import lax
from jax.experimental import pallas as pl
from jax.experimental.pallas import tpu as pltpu
from jax.sharding import PartitionSpec as P

ALL = ("shift", "dom", "eh")
F32 = jnp.float32
BF16 = jnp.bfloat16
SHIFTS, DOMS, EHS = 8, 32, 2
BLK, COLS, LANES = 16, 32, 128
EDGE = 3
INNER = 11
REACH = 10
SPLIT = 7
ROWS = 2 * EDGE * COLS
VM = pltpu.CompilerParams(vmem_limit_bytes=24 * 1024 * 1024)


def flat(s, d, e):
    return (s * DOMS + d) * EHS + e


TURNS = {(0, 1): 1, (1, 0): 2, (1, 1): 3, (2, 0): 4, (16, 1): 5, (17, 0): 6, (17, 1): 7}
POINT_AT = [(0, 0)] + list(TURNS)


def halo_pairs():
    pairs = []
    for s in range(SHIFTS):
        for d in range(DOMS):
            for e in range(EHS):
                source = d - 1 + 2 * e
                if 0 <= source < DOMS:
                    turn = TURNS.get((d, e), 0)
                    pairs.append((flat(s ^ turn, source, e), flat(s, d, e)))
    return pairs


def halves(shape):
    lane = lax.broadcasted_iota(jnp.int32, shape, len(shape) - 1)
    return jnp.where(lane < LANES // 2, 1.0, -1.0).astype(F32)


def split3(x):
    a = x.astype(BF16)
    r = x - a.astype(F32)
    b = r.astype(BF16)
    c = (r - b.astype(F32)).astype(BF16)
    return a, b, c


def quad(a, b, c, d):
    return jnp.concatenate(
        [jnp.concatenate([a, b], 1), jnp.concatenate([c, d], 1)], 0
    )


def tables_kernel(hop_ref, pair_ref, hop_out, pair_out):
    def put(out, at, mat):
        out[at] = jnp.concatenate(split3(mat), 1)

    for t in range(8):
        re, im = hop_ref[t, 0], hop_ref[t, 1]
        ret, imt = re.T, im.T
        bwd = quad(re, im, -im, re)
        fwd = quad(ret, imt, -imt, ret)
        put(hop_out, 3 * t, fwd)
        put(hop_out, 3 * t + 1, bwd)
        put(hop_out, 3 * t + 2, fwd + bwd)
    for t in range(4):
        re, im = pair_ref[t, 0], pair_ref[t, 1]
        ret, imt = re.T, im.T
        put(pair_out, 2 * t, quad(ret, imt, imt, -ret))
        put(pair_out, 2 * t + 1, quad(-re, im, im, re))


def product(lhs, tabs):
    rows = lhs.shape[0] // 3
    both = jnp.concatenate([t[:, : 2 * LANES] for t in tabs], 0)
    third = jnp.concatenate([t[:, 2 * LANES :] for t in tabs], 0)
    big = jnp.dot(lhs, both, preferred_element_type=F32)
    small = jnp.dot(lhs[:rows], third, preferred_element_type=F32)
    small = small + big[2 * rows :, :LANES] + big[rows : 2 * rows, LANES:]
    small = small + (big[:rows, LANES:] + big[rows : 2 * rows, :LANES])
    return big[:rows, :LANES] + small


def crossed(block):
    ref, at = block
    zero = jnp.zeros((COLS, LANES), BF16)
    rows = []
    for part in range(3):
        rows += [ref[at, pl.ds((2 * part + 1) * COLS, COLS)], zero]
    return jnp.concatenate(rows, 0)


def crossed_up(block):
    ref, at = block
    zero = jnp.zeros((COLS, LANES), BF16)
    rows = []
    for part in range(3):
        rows += [zero, ref[at, pl.ds(2 * part * COLS, COLS)]]
    return jnp.concatenate(rows, 0)


def image(blocks, hop_t, pair_t, kinds):
    back2, back1, here, on1, on2, pair = kinds
    lhs = [ref[at] for ref, at in blocks]
    lhs += [crossed(blocks[2]), crossed_up(blocks[2])]
    tabs = [hop_t[3 * back2 + 1], hop_t[3 * back1 + 1], hop_t[3 * here + 2]]
    tabs += [hop_t[3 * on1], hop_t[3 * on2], pair_t[2 * pair], pair_t[2 * pair + 1]]
    return product(jnp.concatenate(lhs, 1), tabs)


def forward_image(blocks, hop_t, pair_t, kinds):
    here, on1, on2, pair = kinds
    lhs = [ref[at] for ref, at in blocks] + [-crossed(blocks[0])]
    tabs = [hop_t[3 * here], hop_t[3 * on1], hop_t[3 * on2], pair_t[2 * pair]]
    return product(jnp.concatenate(lhs, 1), tabs)


def swap(x):
    return pltpu.roll(x, LANES // 2, 1)


def add_pairs(re, im, n, a, b, b_swapped):
    re[n] = a * b if re[n] is None else re[n] + a * b
    im[n] = a * b_swapped if im[n] is None else im[n] + a * b_swapped


def fetch_kernel(
    hop_s, pair_s, shift_ref, weight_ref, hop_ref, pair_ref,
    facts_ref, hop_v, pair_v,
    hop_k, pair_k, shift_v, weight_v, sem,
):
    copies = [
        pltpu.make_async_copy(source, to, sem.at[n])
        for n, (source, to) in enumerate(
            (
                (hop_s, hop_k),
                (pair_s, pair_k),
                (shift_ref, shift_v),
                (weight_ref, weight_v),
                (hop_ref, hop_v),
                (pair_ref, pair_v),
            )
        )
    ]
    for c in copies:
        c.start()
    facts_ref[...] = jnp.zeros_like(facts_ref)
    facts_ref[6:7] = jnp.ones((1, LANES), F32)
    for c in copies:
        c.wait()
    facts_ref[0:3, :BLK] = hop_k[...].astype(F32)
    facts_ref[3:4, :BLK] = pair_k[...].astype(F32)
    facts_ref[4:5, :2] = shift_v[...]
    facts_ref[5:6, :2] = weight_v[...]


def parts_of(elec, hole, sign):
    return jnp.concatenate(split3(jnp.concatenate([elec, hole * sign], 0)), 0)


def inner_kernel(
    win_ref, own_ref, hop_t, pair_t,
    us_ref, g_ref, gs_ref, acc_ref,
    own_s, kind_s, sem,
):
    facts = pltpu.make_async_copy(own_ref.at[pl.ds(ROWS, 8)], own_s, sem)
    facts.start()
    low = lax.axis_index("eh") == 0
    sign = halves((1, LANES))
    for a in range(INNER):
        us_ref[a] = parts_of(win_ref[0, a], win_ref[1, a], sign)
    facts.wait()
    for a in range(INNER - 2):
        for c in range(4):
            kind_s[a, c] = jnp.where(low, own_s[c, a], own_s[c, BLK - INNER + a]).astype(jnp.int32)
    re, im = [None] * 4, [None] * 4
    for k in range(INNER - 4):
        kinds = [kind_s[k, 2], kind_s[k + 1, 1]] + [kind_s[k + 2, c] for c in range(4)]
        g = image([(us_ref, k + n) for n in range(5)], hop_t, pair_t, kinds)
        g_ref[k] = g
        gs_ref[k] = jnp.concatenate(split3(g), 0)
        u = jnp.concatenate([win_ref[0, k + 2], win_ref[1, k + 2] * sign], 0)
        if k + 2 >= SPLIT:
            u, g = jnp.where(low, 0.0, u), jnp.where(low, 0.0, g)
        add_pairs(re, im, 0, u, u, swap(u))
        add_pairs(re, im, 1, u, g, swap(g))
        add_pairs(re, im, 2, g, g, swap(g))
    for k in range(INNER - 6):
        kinds = [kind_s[k + 2, c] for c in range(4)]
        y = forward_image([(gs_ref, k + n) for n in range(3)], hop_t, pair_t, kinds)
        add_pairs(re, im, 3, g_ref[k], y, swap(y))
    for n in range(4):
        acc_ref[2 * n] = re[n]
        acc_ref[2 * n + 1] = im[n]


def outer_side(
    low, win_ref, recv_ref, hop_t, pair_t, us_in, g_in, gs_in, acc_ref,
    us_new, g_ref, gs_new, own, recv, valid,
):
    start = 0 if low else BLK - INNER
    first = -1 if low else SPLIT
    sign = halves((1, LANES))
    edge = [-3, -2, -1] if low else [16, 17, 18]
    for n in range(EDGE):
        elec = recv_ref[pl.ds(n * COLS, COLS)]
        hole = recv_ref[pl.ds((EDGE + n) * COLS, COLS)]
        us_new[n] = parts_of(elec, hole, sign)
    for k in range(INNER - 4):
        g_ref[start + 2 + k - first] = g_in[k]
    images = [-1, 0, 1] if low else [14, 15, 16]
    kinds_of = {}
    for i in range(-3, 2) if low else range(12, 17):
        kinds_of[i] = (own if 0 <= i < BLK else recv)[0, i % BLK]

    def kind(i, c):
        return jnp.bitwise_and(lax.shift_right_logical(kinds_of[i], 3 * c), 7)

    def us(i):
        return (us_new, edge.index(i)) if i in edge else (us_in, i - start)

    def gs(i):
        return (gs_new, images.index(i)) if i in images else (gs_in, i - start - 2)

    re = [acc_ref[2 * n] for n in range(4)]
    im = [acc_ref[2 * n + 1] for n in range(4)]
    for n, i in enumerate(images):
        kinds = [kind(i - 2, 2), kind(i - 1, 1)] + [kind(i, c) for c in range(4)]
        g = image([us(i - 2 + k) for k in range(5)], hop_t, pair_t, kinds)
        own = 0 <= i < BLK
        if not own:
            g = jnp.where(valid, g, 0.0)
        g_ref[i - first] = g
        gs_new[n] = jnp.concatenate(split3(g), 0)
        if own:
            u = jnp.concatenate([win_ref[0, i - start], win_ref[1, i - start] * sign], 0)
            add_pairs(re, im, 0, u, u, swap(u))
            add_pairs(re, im, 1, u, g, swap(g))
            add_pairs(re, im, 2, g, g, swap(g))
    for i in [0, 1] if low else [12, 13, 14]:
        kinds = [kind(i, c) for c in range(4)]
        y = forward_image([gs(i + k) for k in range(3)], hop_t, pair_t, kinds)
        add_pairs(re, im, 3, g_ref[i - first], y, swap(y))
    if low:
        ref, at = gs(1)
        i, y = -1, product(ref[at], [hop_t[3 * kind(-1, 2)]])
    else:
        i = BLK - 1
        lhs = [ref[at] for ref, at in (gs(i), gs(i + 1))] + [-crossed(gs(i))]
        tabs = [hop_t[3 * kind(i, 0)], hop_t[3 * kind(i, 1)], pair_t[2 * kind(i, 3)]]
        y = product(jnp.concatenate(lhs, 1), tabs)
    add_pairs(re, im, 3, g_ref[i - first], y, swap(y))
    rows = []
    for n in range(4):
        s = 1.0 if n in (0, 2) else -1.0
        w = 2.0 if n == 3 else 1.0
        rows.append(w * sign * (re[n][:COLS] + s * re[n][COLS:]))
        rows.append(w * (im[n][:COLS] - s * im[n][COLS:]))
    return rows


def kinds_row(facts):
    row = facts[0:1] + 8.0 * facts[1:2] + 64.0 * facts[2:3] + 512.0 * facts[3:4]
    return row.astype(jnp.int32)


def outer_kernel(
    win_ref, own_ref, recv_ref, hop_t, pair_t, us_in, g_in, gs_in, acc_ref,
    send_ref, img_ref,
    us_new, g_ref, gs_new,
):
    point, eh, dom = (lax.axis_index(x) for x in ("shift", "eh", "dom"))
    own, recv = kinds_row(own_ref[ROWS:]), kinds_row(recv_ref[ROWS:])
    for side in range(2):

        @pl.when(eh == side)
        def _(side=side):
            rows = outer_side(
                side == 0, win_ref, recv_ref, hop_t, pair_t, us_in, g_in, gs_in, acc_ref,
                us_new, g_ref, gs_new, own, recv, dom > 0 if side == 0 else dom < DOMS - 1,
            )
            for k in range(2):
                total = jnp.concatenate(rows[4 * k : 4 * k + 4], 0).T
                send_ref[k : k + 1] = jnp.sum(total, axis=0, keepdims=True)

    low = eh == 0
    sign = halves((1, LANES))
    facts = jnp.where(recv_ref[ROWS + 6 : ROWS + 7] > 0.5, recv_ref[ROWS:], own_ref[ROWS:])
    send_ref[2:3] = facts[4:5] + pltpu.roll(facts[5:6], 2, 1)
    send_ref[3:8] = jnp.zeros((5, LANES), F32)
    first = 2 * jnp.bitwise_and(point, 3) + 1
    for k in range(2):
        g = g_ref[first + k]
        elec, hole = g[:COLS], -sign * g[COLS:]
        img_ref[k] = jnp.where(low, elec, hole)
        send_ref[(1 + 4 * k) * 8 : (5 + 4 * k) * 8] = jnp.where(low, hole, elec)


def cmul(a, b):
    return a[0] * b[0] - a[1] * b[1], a[0] * b[1] + a[1] * b[0]


def cadd(a, b):
    return a[0] + b[0], a[1] + b[1]


def cdiv(a, b):
    denom = jnp.maximum(b[0] * b[0] + b[1] * b[1], 1.0)
    return (a[0] * b[0] + a[1] * b[1]) / denom, (a[1] * b[0] - a[0] * b[1]) / denom


def combine_kernel(mom_ref, right_ref, img_ref, sent_ref, out_ref):
    total = jnp.sum(mom_ref[...], axis=0)
    pts = jnp.concatenate([mom_ref[d, 2 + e : 3 + e] for d, e in POINT_AT], 0)

    def moment(n):
        row = total[n // 2 : n // 2 + 1]
        at = (n % 2) * 64
        return tuple(
            jnp.broadcast_to(row[:, at + k * COLS : at + (k + 1) * COLS], (SHIFTS, COLS))
            for k in range(2)
        )

    def param(n):
        return tuple(
            jnp.broadcast_to(pts[:, n + k : n + k + 1], (SHIFTS, COLS)) for k in range(2)
        )

    m0, m1, m2, m3 = (moment(n) for n in range(4))
    z, w = param(0), param(2)

    def minus(a, b):
        return a[0] - b[0], a[1] - b[1]

    def twice(a):
        return 2.0 * a[0], 2.0 * a[1]

    a0 = cdiv(m0, minus(cmul(z, m0), m1))
    az = cmul(a0, z)
    s = (1.0 - az[0], -az[1])
    s2, sa, aa = cmul(s, s), cmul(s, a0), cmul(a0, a0)
    rho = cadd(cadd(cmul(s2, m0), twice(cmul(sa, m1))), cmul(aa, m2))
    c = cadd(s, cdiv(rho, m0))
    cc, ca = cmul(c, c), cmul(c, a0)
    pp = cadd(cadd(cmul(cc, m0), twice(cmul(ca, m1))), cmul(aa, m2))
    php = cadd(cadd(cmul(cc, m1), twice(cmul(ca, m2))), cmul(aa, m3))
    a1 = cdiv(rho, minus(cmul(z, pp), php))
    c0 = cmul(w, cadd(a0, cmul(a1, c)))
    c1 = cmul(w, cmul(a1, a0))
    rows = [jnp.sum(x, axis=0, keepdims=True) for x in (*c0, *c1)]
    stack = jnp.concatenate(rows + [jnp.zeros((4, COLS), F32)], 0)
    stack = jnp.concatenate([stack, jnp.zeros((8, LANES - COLS), F32)], 1)
    cols = stack.T[:COLS]
    sign = -halves((1, LANES))
    point = lax.axis_index("shift")
    holder = (point >= SHIFTS // 2).astype(jnp.int32)
    mine = lax.axis_index("eh") == holder
    for k in range(2):
        b = right_ref[0, 2 * point + k]
        g = jnp.where(mine, img_ref[k], sent_ref[holder, (1 + 4 * k) * 8 : (5 + 4 * k) * 8])
        out = cols[:, 0:1] * b + cols[:, 1:2] * (pltpu.roll(b, LANES // 2, 1) * sign)
        out = out + cols[:, 2:3] * g + cols[:, 3:4] * (pltpu.roll(g, LANES // 2, 1) * sign)
        out_ref[0, k] = out


def body(right_side, shifts, quad_weights, hop_table, pair_table, hop_type, pair_type):
    vmem = pl.BlockSpec(memory_space=pltpu.VMEM)
    low = lax.axis_index("eh") == 0
    inputs = (hop_type.T, pair_type[None], shifts, quad_weights, hop_table, pair_table)
    facts, hops, pairs = pl.pallas_call(
        fetch_kernel,
        out_shape=[
            jax.ShapeDtypeStruct((8, LANES), F32),
            jax.ShapeDtypeStruct(hop_table.shape, F32),
            jax.ShapeDtypeStruct(pair_table.shape, F32),
        ],
        in_specs=[pl.BlockSpec(memory_space=pltpu.HBM)] * 6,
        out_specs=[vmem] * 3,
        scratch_shapes=[
            pltpu.VMEM((3, BLK), jnp.int32),
            pltpu.VMEM((1, BLK), jnp.int32),
            pltpu.VMEM((1, 2), F32),
            pltpu.VMEM((1, 2), F32),
            pltpu.SemaphoreType.DMA((6,)),
        ],
        compiler_params=VM,
        name="fetch",
    )(*(pltpu.with_memory_space_constraint(x, pltpu.HBM) for x in inputs))
    both = lax.all_gather(right_side[0], "eh")
    edge = lax.dynamic_slice_in_dim(both, jnp.where(low, BLK - EDGE, 0), EDGE, 1)
    own = jnp.concatenate([edge.reshape(ROWS, LANES), facts], 0)
    recv = lax.ppermute(own, ALL, halo_pairs())
    hop_t, pair_t = pl.pallas_call(
        tables_kernel,
        out_shape=[
            jax.ShapeDtypeStruct((24, LANES, 3 * LANES), BF16),
            jax.ShapeDtypeStruct((8, LANES, 3 * LANES), BF16),
        ],
        in_specs=[vmem] * 2,
        out_specs=[vmem] * 2,
        compiler_params=VM,
        name="tables",
    )(hops, pairs)
    win = lax.dynamic_slice_in_dim(both, jnp.where(low, 0, BLK - INNER), INNER, 1)
    us, g, gs, acc = pl.pallas_call(
        inner_kernel,
        out_shape=[
            jax.ShapeDtypeStruct((INNER, 6 * COLS, LANES), BF16),
            jax.ShapeDtypeStruct((INNER - 4, 2 * COLS, LANES), F32),
            jax.ShapeDtypeStruct((INNER - 4, 6 * COLS, LANES), BF16),
            jax.ShapeDtypeStruct((8, 2 * COLS, LANES), F32),
        ],
        in_specs=[vmem] * 4,
        out_specs=[vmem] * 4,
        scratch_shapes=[
            pltpu.SMEM((8, LANES), F32),
            pltpu.SMEM((INNER, 4), jnp.int32),
            pltpu.SemaphoreType.DMA,
        ],
        compiler_params=VM,
        name="inner",
    )(win, own, hop_t, pair_t)
    send, img = pl.pallas_call(
        outer_kernel,
        out_shape=[
            jax.ShapeDtypeStruct((72, LANES), F32),
            jax.ShapeDtypeStruct((2, COLS, LANES), F32),
        ],
        in_specs=[vmem] * 9,
        out_specs=[vmem] * 2,
        scratch_shapes=[
            pltpu.VMEM((EDGE, 6 * COLS, LANES), BF16),
            pltpu.VMEM((REACH, 2 * COLS, LANES), F32),
            pltpu.VMEM((EDGE, 6 * COLS, LANES), BF16),
        ],
        compiler_params=VM,
        name="outer",
    )(win, own, recv, hop_t, pair_t, us, g, gs, acc)
    sent = lax.all_gather(send, "eh")
    mom = jnp.concatenate([sent[0, :2] + sent[1, :2], sent[:, 2]], 0)
    mom = jnp.broadcast_to(mom[None], (DOMS, 4, LANES))
    parts = lax.all_to_all(mom, "dom", 0, 0)
    return pl.pallas_call(
        combine_kernel,
        out_shape=jax.ShapeDtypeStruct((1, 2, COLS, LANES), F32),
        in_specs=[vmem] * 4,
        out_specs=vmem,
        compiler_params=VM,
        name="combine",
    )(parts, right_side, img, sent)


def solution(mesh):
    placed = (
        P("eh", "dom", None, None),
        P("shift", None),
        P("shift", None),
        P(),
        P(),
        P("dom", None),
        P("dom"),
    )
    return jax.shard_map(
        body,
        mesh=mesh,
        in_specs=placed,
        out_specs=P("eh", ("dom", "shift"), None, None),
        check_vma=False,
    )
```

```python
import jax
import jax.numpy as jnp
from jax import lax
from jax.experimental import pallas as pl
from jax.experimental.pallas import tpu as pltpu
from jax.sharding import PartitionSpec as P

ALL = ("shift", "dom", "eh")
F32 = jnp.float32
BF16 = jnp.bfloat16
SHIFTS, DOMS, EHS = 8, 32, 2
BLK, COLS, LANES = 16, 32, 128
EDGE = 3
INNER = 11
REACH = 10
SPLIT = 7
ROWS = 2 * EDGE * COLS
VM = pltpu.CompilerParams(vmem_limit_bytes=24 * 1024 * 1024)


def flat(s, d, e):
    return (s * DOMS + d) * EHS + e


TURNS = {(0, 1): 1, (1, 0): 2, (1, 1): 3, (2, 0): 4, (16, 1): 5, (17, 0): 6, (17, 1): 7}
POINT_AT = [(0, 0)] + list(TURNS)


def halo_pairs():
    pairs = []
    for s in range(SHIFTS):
        for d in range(DOMS):
            for e in range(EHS):
                source = d - 1 + 2 * e
                if 0 <= source < DOMS:
                    turn = TURNS.get((d, e), 0)
                    pairs.append((flat(s ^ turn, source, e), flat(s, d, e)))
    return pairs


def halves(shape):
    lane = lax.broadcasted_iota(jnp.int32, shape, len(shape) - 1)
    return jnp.where(lane < LANES // 2, 1.0, -1.0).astype(F32)


def split3(x):
    a = x.astype(BF16)
    r = x - a.astype(F32)
    b = r.astype(BF16)
    c = (r - b.astype(F32)).astype(BF16)
    return a, b, c


def quad(a, b, c, d):
    return jnp.concatenate(
        [jnp.concatenate([a, b], 1), jnp.concatenate([c, d], 1)], 0
    )


def tables_kernel(hop_ref, pair_ref, hop_out, pair_out):
    def put(out, at, mat):
        out[at] = jnp.concatenate(split3(mat), 1)

    for t in range(8):
        re, im = hop_ref[t, 0], hop_ref[t, 1]
        ret, imt = re.T, im.T
        bwd = quad(re, im, -im, re)
        fwd = quad(ret, imt, -imt, ret)
        put(hop_out, 3 * t, fwd)
        put(hop_out, 3 * t + 1, bwd)
        put(hop_out, 3 * t + 2, fwd + bwd)
    for t in range(4):
        re, im = pair_ref[t, 0], pair_ref[t, 1]
        ret, imt = re.T, im.T
        put(pair_out, 2 * t, quad(ret, imt, imt, -ret))
        put(pair_out, 2 * t + 1, quad(-re, im, im, re))


def product(lhs, tabs):
    rows = lhs.shape[0] // 3
    both = jnp.concatenate([t[:, : 2 * LANES] for t in tabs], 0)
    third = jnp.concatenate([t[:, 2 * LANES :] for t in tabs], 0)
    big = jnp.dot(lhs, both, preferred_element_type=F32)
    small = jnp.dot(lhs[:rows], third, preferred_element_type=F32)
    small = small + big[2 * rows :, :LANES] + big[rows : 2 * rows, LANES:]
    small = small + (big[:rows, LANES:] + big[rows : 2 * rows, :LANES])
    return big[:rows, :LANES] + small


def crossed(block):
    ref, at = block
    zero = jnp.zeros((COLS, LANES), BF16)
    rows = []
    for part in range(3):
        rows += [ref[at, pl.ds((2 * part + 1) * COLS, COLS)], zero]
    return jnp.concatenate(rows, 0)


def crossed_up(block):
    ref, at = block
    zero = jnp.zeros((COLS, LANES), BF16)
    rows = []
    for part in range(3):
        rows += [zero, ref[at, pl.ds(2 * part * COLS, COLS)]]
    return jnp.concatenate(rows, 0)


def image(blocks, hop_t, pair_t, kinds):
    back2, back1, here, on1, on2, pair = kinds
    lhs = [ref[at] for ref, at in blocks]
    lhs += [crossed(blocks[2]), crossed_up(blocks[2])]
    tabs = [hop_t[3 * back2 + 1], hop_t[3 * back1 + 1], hop_t[3 * here + 2]]
    tabs += [hop_t[3 * on1], hop_t[3 * on2], pair_t[2 * pair], pair_t[2 * pair + 1]]
    return product(jnp.concatenate(lhs, 1), tabs)


def forward_image(blocks, hop_t, pair_t, kinds):
    here, on1, on2, pair = kinds
    lhs = [ref[at] for ref, at in blocks] + [-crossed(blocks[0])]
    tabs = [hop_t[3 * here], hop_t[3 * on1], hop_t[3 * on2], pair_t[2 * pair]]
    return product(jnp.concatenate(lhs, 1), tabs)


def swap(x):
    return pltpu.roll(x, LANES // 2, 1)


def add_pairs(re, im, n, a, b, b_swapped):
    re[n] = a * b if re[n] is None else re[n] + a * b
    im[n] = a * b_swapped if im[n] is None else im[n] + a * b_swapped


def fetch_kernel(
    hop_s, pair_s, shift_ref, weight_ref, hop_ref, pair_ref, right_ref,
    facts_ref, hop_v, pair_v, mine_ref,
    hop_k, pair_k, shift_v, weight_v, sem,
):
    copies = [
        pltpu.make_async_copy(source, to, sem.at[n])
        for n, (source, to) in enumerate(
            (
                (hop_s, hop_k),
                (pair_s, pair_k),
                (shift_ref, shift_v),
                (weight_ref, weight_v),
                (hop_ref, hop_v),
                (pair_ref, pair_v),
                (right_ref, mine_ref),
            )
        )
    ]
    for c in copies:
        c.start()
    facts_ref[...] = jnp.zeros_like(facts_ref)
    facts_ref[6:7] = jnp.ones((1, LANES), F32)
    for c in copies:
        c.wait()
    facts_ref[0:3, :BLK] = hop_k[...].astype(F32)
    facts_ref[3:4, :BLK] = pair_k[...].astype(F32)
    facts_ref[4:5, :2] = shift_v[...]
    facts_ref[5:6, :2] = weight_v[...]


def parts_of(elec, hole, sign):
    return jnp.concatenate(split3(jnp.concatenate([elec, hole * sign], 0)), 0)


def inner_kernel(
    win_ref, own_ref, hop_t, pair_t,
    us_ref, g_ref, gs_ref, acc_ref,
    own_s, kind_s, sem,
):
    facts = pltpu.make_async_copy(own_ref.at[pl.ds(ROWS, 8)], own_s, sem)
    facts.start()
    low = lax.axis_index("eh") == 0
    sign = halves((1, LANES))

    def both(a):
        x, y = win_ref[0, a], win_ref[1, a]
        return jnp.where(low, x, y), jnp.where(low, y, x)

    for a in range(INNER):
        us_ref[a] = parts_of(*both(a), sign)
    facts.wait()
    for a in range(INNER - 2):
        for c in range(4):
            kind_s[a, c] = jnp.where(low, own_s[c, a], own_s[c, BLK - INNER + a]).astype(jnp.int32)
    re, im = [None] * 4, [None] * 4
    for k in range(INNER - 4):
        kinds = [kind_s[k, 2], kind_s[k + 1, 1]] + [kind_s[k + 2, c] for c in range(4)]
        g = image([(us_ref, k + n) for n in range(5)], hop_t, pair_t, kinds)
        g_ref[k] = g
        gs_ref[k] = jnp.concatenate(split3(g), 0)
        elec, hole = both(k + 2)
        u = jnp.concatenate([elec, hole * sign], 0)
        if k + 2 >= SPLIT:
            u, g = jnp.where(low, 0.0, u), jnp.where(low, 0.0, g)
        add_pairs(re, im, 0, u, u, swap(u))
        add_pairs(re, im, 1, u, g, swap(g))
        add_pairs(re, im, 2, g, g, swap(g))
    for k in range(INNER - 6):
        kinds = [kind_s[k + 2, c] for c in range(4)]
        y = forward_image([(gs_ref, k + n) for n in range(3)], hop_t, pair_t, kinds)
        add_pairs(re, im, 3, g_ref[k], y, swap(y))
    for n in range(4):
        acc_ref[2 * n] = re[n]
        acc_ref[2 * n + 1] = im[n]


def outer_side(
    low, win_ref, recv_ref, hop_t, pair_t, us_in, g_in, gs_in, acc_ref,
    us_new, g_ref, gs_new, own, recv, valid,
):
    start = 0 if low else BLK - INNER
    first = -1 if low else SPLIT
    sign = halves((1, LANES))
    edge = [-3, -2, -1] if low else [16, 17, 18]
    e, h = (0, 1) if low else (1, 0)
    for n in range(EDGE):
        elec = recv_ref[pl.ds((e * EDGE + n) * COLS, COLS)]
        hole = recv_ref[pl.ds((h * EDGE + n) * COLS, COLS)]
        us_new[n] = parts_of(elec, hole, sign)
    for k in range(INNER - 4):
        g_ref[start + 2 + k - first] = g_in[k]
    images = [-1, 0, 1] if low else [14, 15, 16]
    kinds_of = {}
    for i in range(-3, 2) if low else range(12, 17):
        kinds_of[i] = (own if 0 <= i < BLK else recv)[0, i % BLK]

    def kind(i, c):
        return jnp.bitwise_and(lax.shift_right_logical(kinds_of[i], 3 * c), 7)

    def us(i):
        return (us_new, edge.index(i)) if i in edge else (us_in, i - start)

    def gs(i):
        return (gs_new, images.index(i)) if i in images else (gs_in, i - start - 2)

    re = [acc_ref[2 * n] for n in range(4)]
    im = [acc_ref[2 * n + 1] for n in range(4)]
    for n, i in enumerate(images):
        kinds = [kind(i - 2, 2), kind(i - 1, 1)] + [kind(i, c) for c in range(4)]
        g = image([us(i - 2 + k) for k in range(5)], hop_t, pair_t, kinds)
        own = 0 <= i < BLK
        if not own:
            g = jnp.where(valid, g, 0.0)
        g_ref[i - first] = g
        gs_new[n] = jnp.concatenate(split3(g), 0)
        if own:
            u = jnp.concatenate([win_ref[e, i - start], win_ref[h, i - start] * sign], 0)
            add_pairs(re, im, 0, u, u, swap(u))
            add_pairs(re, im, 1, u, g, swap(g))
            add_pairs(re, im, 2, g, g, swap(g))
    for i in [0, 1] if low else [12, 13, 14]:
        kinds = [kind(i, c) for c in range(4)]
        y = forward_image([gs(i + k) for k in range(3)], hop_t, pair_t, kinds)
        add_pairs(re, im, 3, g_ref[i - first], y, swap(y))
    if low:
        ref, at = gs(1)
        i, y = -1, product(ref[at], [hop_t[3 * kind(-1, 2)]])
    else:
        i = BLK - 1
        lhs = [ref[at] for ref, at in (gs(i), gs(i + 1))] + [-crossed(gs(i))]
        tabs = [hop_t[3 * kind(i, 0)], hop_t[3 * kind(i, 1)], pair_t[2 * kind(i, 3)]]
        y = product(jnp.concatenate(lhs, 1), tabs)
    add_pairs(re, im, 3, g_ref[i - first], y, swap(y))
    rows = []
    for n in range(4):
        s = 1.0 if n in (0, 2) else -1.0
        w = 2.0 if n == 3 else 1.0
        rows.append(w * sign * (re[n][:COLS] + s * re[n][COLS:]))
        rows.append(w * (im[n][:COLS] - s * im[n][COLS:]))
    return rows


def kinds_row(facts):
    row = facts[0:1] + 8.0 * facts[1:2] + 64.0 * facts[2:3] + 512.0 * facts[3:4]
    return row.astype(jnp.int32)


def outer_kernel(
    win_ref, own_ref, recv_ref, hop_t, pair_t, us_in, g_in, gs_in, acc_ref,
    send_ref, img_ref,
    us_new, g_ref, gs_new,
):
    point, eh, dom = (lax.axis_index(x) for x in ("shift", "eh", "dom"))
    own, recv = kinds_row(own_ref[ROWS:]), kinds_row(recv_ref[ROWS:])
    for side in range(2):

        @pl.when(eh == side)
        def _(side=side):
            rows = outer_side(
                side == 0, win_ref, recv_ref, hop_t, pair_t, us_in, g_in, gs_in, acc_ref,
                us_new, g_ref, gs_new, own, recv, dom > 0 if side == 0 else dom < DOMS - 1,
            )
            for k in range(2):
                total = jnp.concatenate(rows[4 * k : 4 * k + 4], 0).T
                send_ref[k : k + 1] = jnp.sum(total, axis=0, keepdims=True)

    low = eh == 0
    sign = halves((1, LANES))
    facts = jnp.where(recv_ref[ROWS + 6 : ROWS + 7] > 0.5, recv_ref[ROWS:], own_ref[ROWS:])
    params = facts[4:5] + pltpu.roll(facts[5:6], 2, 1)
    send_ref[2:3] = jnp.where(low, params, pltpu.roll(params, 4, 1))
    send_ref[3:8] = jnp.zeros((5, LANES), F32)
    first = 2 * jnp.bitwise_and(point, 3) + 1
    for k in range(2):
        g = g_ref[first + k]
        elec, hole = g[:COLS], -sign * g[COLS:]
        img_ref[k] = jnp.where(low, elec, hole)
        send_ref[(1 + 4 * k) * 8 : (5 + 4 * k) * 8] = jnp.where(low, hole, elec)


def cmul(a, b):
    return a[0] * b[0] - a[1] * b[1], a[0] * b[1] + a[1] * b[0]


def cadd(a, b):
    return a[0] + b[0], a[1] + b[1]


def cdiv(a, b):
    denom = jnp.maximum(b[0] * b[0] + b[1] * b[1], 1.0)
    scale = 1.0 / denom
    return (a[0] * b[0] + a[1] * b[1]) * scale, (a[1] * b[0] - a[0] * b[1]) * scale


def combine_kernel(mom_ref, right_ref, img_ref, sent_ref, out_ref):
    total = jnp.sum(mom_ref[:, :, : 2 * LANES], axis=0)
    total = jnp.concatenate([total[:, :LANES], total[:, LANES:]], 0)
    pts = [[mom_ref[d, :, 2 * LANES :] for d, e in POINT_AT if e == core] for core in range(EHS)]
    pts = [jnp.concatenate(x, 0) for x in pts]
    pts = jnp.concatenate([pts[0], pltpu.roll(pts[1], LANES - 4, 1)], 0)

    def moment(n):
        row = total[n // 2 : n // 2 + 1]
        at = (n % 2) * 64
        return tuple(
            jnp.broadcast_to(row[:, at + k * COLS : at + (k + 1) * COLS], (SHIFTS, COLS))
            for k in range(2)
        )

    def param(n):
        return tuple(
            jnp.broadcast_to(pts[:, n + k : n + k + 1], (SHIFTS, COLS)) for k in range(2)
        )

    m0, m1, m2, m3 = (moment(n) for n in range(4))
    z, w = param(0), param(2)

    def minus(a, b):
        return a[0] - b[0], a[1] - b[1]

    def twice(a):
        return 2.0 * a[0], 2.0 * a[1]

    a0 = cdiv(m0, minus(cmul(z, m0), m1))
    az = cmul(a0, z)
    s = (1.0 - az[0], -az[1])
    s2, sa, aa = cmul(s, s), cmul(s, a0), cmul(a0, a0)
    rho = cadd(cadd(cmul(s2, m0), twice(cmul(sa, m1))), cmul(aa, m2))
    c = cadd(s, cdiv(rho, m0))
    cc, ca = cmul(c, c), cmul(c, a0)
    pp = cadd(cadd(cmul(cc, m0), twice(cmul(ca, m1))), cmul(aa, m2))
    php = cadd(cadd(cmul(cc, m1), twice(cmul(ca, m2))), cmul(aa, m3))
    a1 = cdiv(rho, minus(cmul(z, pp), php))
    c0 = cmul(w, cadd(a0, cmul(a1, c)))
    c1 = cmul(w, cmul(a1, a0))
    rows = [jnp.sum(x, axis=0, keepdims=True) for x in (*c0, *c1)]
    stack = jnp.concatenate(rows + [jnp.zeros((4, COLS), F32)], 0)
    stack = jnp.concatenate([stack, jnp.zeros((8, LANES - COLS), F32)], 1)
    cols = stack.T[:COLS]
    sign = -halves((1, LANES))
    point = lax.axis_index("shift")
    holder = (point >= SHIFTS // 2).astype(jnp.int32)
    mine = lax.axis_index("eh") == holder
    for k in range(2):
        b = right_ref[2 * point + k]
        g = jnp.where(mine, img_ref[k], sent_ref[holder, (1 + 4 * k) * 8 : (5 + 4 * k) * 8])
        out = cols[:, 0:1] * b + cols[:, 1:2] * (pltpu.roll(b, LANES // 2, 1) * sign)
        out = out + cols[:, 2:3] * g + cols[:, 3:4] * (pltpu.roll(g, LANES // 2, 1) * sign)
        out_ref[0, k] = out


def body(right_side, shifts, quad_weights, hop_table, pair_table, hop_type, pair_type):
    vmem = pl.BlockSpec(memory_space=pltpu.VMEM)
    low = lax.axis_index("eh") == 0
    right = right_side[0]
    inputs = (hop_type.T, pair_type[None], shifts, quad_weights, hop_table, pair_table, right)
    other = lax.ppermute(right, "eh", [(0, 1), (1, 0)])
    facts, hops, pairs, mine = pl.pallas_call(
        fetch_kernel,
        out_shape=[
            jax.ShapeDtypeStruct((8, LANES), F32),
            jax.ShapeDtypeStruct(hop_table.shape, F32),
            jax.ShapeDtypeStruct(pair_table.shape, F32),
            jax.ShapeDtypeStruct(right.shape, F32),
        ],
        in_specs=[pl.BlockSpec(memory_space=pltpu.HBM)] * 7,
        out_specs=[vmem] * 4,
        scratch_shapes=[
            pltpu.VMEM((3, BLK), jnp.int32),
            pltpu.VMEM((1, BLK), jnp.int32),
            pltpu.VMEM((1, 2), F32),
            pltpu.VMEM((1, 2), F32),
            pltpu.SemaphoreType.DMA((7,)),
        ],
        compiler_params=VM,
        name="fetch",
    )(*(pltpu.with_memory_space_constraint(x, pltpu.HBM) for x in inputs))
    at = jnp.where(low, BLK - EDGE, 0)
    edge = [lax.dynamic_slice_in_dim(x, at, EDGE, 0).reshape(-1, LANES) for x in (mine, other)]
    own = jnp.concatenate([*edge, facts], 0)
    own, hops, pairs = lax.optimization_barrier((own, hops, pairs))
    recv = lax.ppermute(own, ALL, halo_pairs())
    hop_t, pair_t = pl.pallas_call(
        tables_kernel,
        out_shape=[
            jax.ShapeDtypeStruct((24, LANES, 3 * LANES), BF16),
            jax.ShapeDtypeStruct((8, LANES, 3 * LANES), BF16),
        ],
        in_specs=[vmem] * 2,
        out_specs=[vmem] * 2,
        compiler_params=VM,
        name="tables",
    )(hops, pairs)
    at = jnp.where(low, 0, BLK - INNER)
    win = jnp.stack([lax.dynamic_slice_in_dim(x, at, INNER, 0) for x in (mine, other)])
    us, g, gs, acc = pl.pallas_call(
        inner_kernel,
        out_shape=[
            jax.ShapeDtypeStruct((INNER, 6 * COLS, LANES), BF16),
            jax.ShapeDtypeStruct((INNER - 4, 2 * COLS, LANES), F32),
            jax.ShapeDtypeStruct((INNER - 4, 6 * COLS, LANES), BF16),
            jax.ShapeDtypeStruct((8, 2 * COLS, LANES), F32),
        ],
        in_specs=[vmem] * 4,
        out_specs=[vmem] * 4,
        scratch_shapes=[
            pltpu.SMEM((8, LANES), F32),
            pltpu.SMEM((INNER, 4), jnp.int32),
            pltpu.SemaphoreType.DMA,
        ],
        compiler_params=VM,
        name="inner",
    )(win, own, hop_t, pair_t)
    send, img = pl.pallas_call(
        outer_kernel,
        out_shape=[
            jax.ShapeDtypeStruct((72, LANES), F32),
            jax.ShapeDtypeStruct((2, COLS, LANES), F32),
        ],
        in_specs=[vmem] * 9,
        out_specs=[vmem] * 2,
        scratch_shapes=[
            pltpu.VMEM((EDGE, 6 * COLS, LANES), BF16),
            pltpu.VMEM((REACH, 2 * COLS, LANES), F32),
            pltpu.VMEM((EDGE, 6 * COLS, LANES), BF16),
        ],
        compiler_params=VM,
        name="outer",
    )(win, own, recv, hop_t, pair_t, us, g, gs, acc)
    sent = lax.all_gather(send, "eh")
    mom = (sent[0, :3] + sent[1, :3]).reshape(1, 1, 3 * LANES)
    mom = jnp.broadcast_to(mom, (DOMS, 1, 3 * LANES))
    parts = lax.all_to_all(mom, "dom", 0, 0)
    return pl.pallas_call(
        combine_kernel,
        out_shape=jax.ShapeDtypeStruct((1, 2, COLS, LANES), F32),
        in_specs=[vmem] * 4,
        out_specs=vmem,
        compiler_params=VM,
        name="combine",
    )(parts, mine, img, sent)


def solution(mesh):
    placed = (
        P("eh", "dom", None, None),
        P("shift", None),
        P("shift", None),
        P(),
        P(),
        P("dom", None),
        P("dom"),
    )
    return jax.shard_map(
        body,
        mesh=mesh,
        in_specs=placed,
        out_specs=P("eh", ("dom", "shift"), None, None),
        check_vma=False,
    )
```

```python
import jax
import jax.numpy as jnp
from jax import lax
from jax.experimental import pallas as pl
from jax.experimental.pallas import tpu as pltpu
from jax.sharding import PartitionSpec as P

ALL = ("shift", "dom", "eh")
F32 = jnp.float32
BF16 = jnp.bfloat16
SHIFTS, DOMS, EHS = 8, 32, 2
BLK, COLS, LANES = 16, 32, 128
EDGE = 3
INNER = 11
REACH = 10
SPLIT = 7
ROWS = 2 * EDGE * COLS
VM = pltpu.CompilerParams(vmem_limit_bytes=24 * 1024 * 1024)


def flat(s, d, e):
    return (s * DOMS + d) * EHS + e


TURNS = {(1, 0): 1, (2, 0): 2, (3, 0): 3, (17, 0): 4, (18, 0): 5, (19, 0): 6, (4, 0): 7}
POINT_AT = [(0, 0)] + list(TURNS)


def halo_pairs():
    pairs = []
    for s in range(SHIFTS):
        for d in range(DOMS):
            for e in range(EHS):
                source = d - 1 + 2 * e
                if 0 <= source < DOMS:
                    turn = TURNS.get((d, e), 0)
                    pairs.append((flat(s ^ turn, source, e), flat(s, d, e)))
    return pairs


def halves(shape):
    lane = lax.broadcasted_iota(jnp.int32, shape, len(shape) - 1)
    return jnp.where(lane < LANES // 2, 1.0, -1.0).astype(F32)


def split3(x):
    a = x.astype(BF16)
    r = x - a.astype(F32)
    b = r.astype(BF16)
    c = (r - b.astype(F32)).astype(BF16)
    return a, b, c


def quad(a, b, c, d):
    return jnp.concatenate(
        [jnp.concatenate([a, b], 1), jnp.concatenate([c, d], 1)], 0
    )


def tables_kernel(hop_ref, pair_ref, hop_out, pair_out):
    def put(out, at, mat):
        out[at] = jnp.concatenate(split3(mat), 1)

    for t in range(8):
        re, im = hop_ref[t, 0], hop_ref[t, 1]
        ret, imt = re.T, im.T
        bwd = quad(re, im, -im, re)
        fwd = quad(ret, imt, -imt, ret)
        put(hop_out, 3 * t, fwd)
        put(hop_out, 3 * t + 1, bwd)
        put(hop_out, 3 * t + 2, fwd + bwd)
    for t in range(4):
        re, im = pair_ref[t, 0], pair_ref[t, 1]
        ret, imt = re.T, im.T
        put(pair_out, 2 * t, quad(ret, imt, imt, -ret))
        put(pair_out, 2 * t + 1, quad(-re, im, im, re))


def product(lhs, tabs):
    rows = lhs.shape[0] // 3
    both = jnp.concatenate([t[:, : 2 * LANES] for t in tabs], 0)
    third = jnp.concatenate([t[:, 2 * LANES :] for t in tabs], 0)
    big = jnp.dot(lhs, both, preferred_element_type=F32)
    small = jnp.dot(lhs[:rows], third, preferred_element_type=F32)
    small = small + big[2 * rows :, :LANES] + big[rows : 2 * rows, LANES:]
    small = small + (big[:rows, LANES:] + big[rows : 2 * rows, :LANES])
    return big[:rows, :LANES] + small


def crossed(block):
    ref, at = block
    zero = jnp.zeros((COLS, LANES), BF16)
    rows = []
    for part in range(3):
        rows += [ref[at, pl.ds((2 * part + 1) * COLS, COLS)], zero]
    return jnp.concatenate(rows, 0)


def crossed_up(block):
    ref, at = block
    zero = jnp.zeros((COLS, LANES), BF16)
    rows = []
    for part in range(3):
        rows += [zero, ref[at, pl.ds(2 * part * COLS, COLS)]]
    return jnp.concatenate(rows, 0)


def image(blocks, hop_t, pair_t, kinds):
    back2, back1, here, on1, on2, pair = kinds
    lhs = [ref[at] for ref, at in blocks]
    lhs += [crossed(blocks[2]), crossed_up(blocks[2])]
    tabs = [hop_t[3 * back2 + 1], hop_t[3 * back1 + 1], hop_t[3 * here + 2]]
    tabs += [hop_t[3 * on1], hop_t[3 * on2], pair_t[2 * pair], pair_t[2 * pair + 1]]
    return product(jnp.concatenate(lhs, 1), tabs)


def forward_image(blocks, hop_t, pair_t, kinds):
    here, on1, on2, pair = kinds
    lhs = [ref[at] for ref, at in blocks] + [-crossed(blocks[0])]
    tabs = [hop_t[3 * here], hop_t[3 * on1], hop_t[3 * on2], pair_t[2 * pair]]
    return product(jnp.concatenate(lhs, 1), tabs)


def swap(x):
    return pltpu.roll(x, LANES // 2, 1)


def add_pairs(re, im, n, a, b, b_swapped):
    re[n] = a * b if re[n] is None else re[n] + a * b
    im[n] = a * b_swapped if im[n] is None else im[n] + a * b_swapped


def fetch_kernel(
    hop_s, pair_s, shift_ref, weight_ref, hop_ref, pair_ref, right_ref,
    facts_ref, hop_v, pair_v, mine_ref,
    hop_k, pair_k, shift_v, weight_v, sem,
):
    copies = [
        pltpu.make_async_copy(source, to, sem.at[n])
        for n, (source, to) in enumerate(
            (
                (hop_s, hop_k),
                (pair_s, pair_k),
                (shift_ref, shift_v),
                (weight_ref, weight_v),
                (hop_ref, hop_v),
                (pair_ref, pair_v),
                (right_ref, mine_ref),
            )
        )
    ]
    for c in copies:
        c.start()
    facts_ref[...] = jnp.zeros_like(facts_ref)
    facts_ref[6:7] = jnp.ones((1, LANES), F32)
    for c in copies:
        c.wait()
    facts_ref[0:3, :BLK] = hop_k[...].astype(F32)
    facts_ref[3:4, :BLK] = pair_k[...].astype(F32)
    facts_ref[4:5, :2] = shift_v[...]
    facts_ref[5:6, :2] = weight_v[...]


def parts_of(elec, hole, sign):
    return jnp.concatenate(split3(jnp.concatenate([elec, hole * sign], 0)), 0)


def inner_kernel(
    win_ref, own_ref, hop_t, pair_t,
    us_ref, g_ref, gs_ref, acc_ref,
    own_s, kind_s, sem,
):
    facts = pltpu.make_async_copy(own_ref.at[pl.ds(ROWS, 8)], own_s, sem)
    facts.start()
    low = lax.axis_index("eh") == 0
    sign = halves((1, LANES))

    def both(a):
        x, y = win_ref[0, a], win_ref[1, a]
        return jnp.where(low, x, y), jnp.where(low, y, x)

    for a in range(INNER):
        us_ref[a] = parts_of(*both(a), sign)
    facts.wait()
    for a in range(INNER - 2):
        for c in range(4):
            kind_s[a, c] = jnp.where(low, own_s[c, a], own_s[c, BLK - INNER + a]).astype(jnp.int32)
    re, im = [None] * 4, [None] * 4
    for k in range(INNER - 4):
        kinds = [kind_s[k, 2], kind_s[k + 1, 1]] + [kind_s[k + 2, c] for c in range(4)]
        g = image([(us_ref, k + n) for n in range(5)], hop_t, pair_t, kinds)
        g_ref[k] = g
        gs_ref[k] = jnp.concatenate(split3(g), 0)
        elec, hole = both(k + 2)
        u = jnp.concatenate([elec, hole * sign], 0)
        if k + 2 >= SPLIT:
            u, g = jnp.where(low, 0.0, u), jnp.where(low, 0.0, g)
        add_pairs(re, im, 0, u, u, swap(u))
        add_pairs(re, im, 1, u, g, swap(g))
        add_pairs(re, im, 2, g, g, swap(g))
    for k in range(INNER - 6):
        kinds = [kind_s[k + 2, c] for c in range(4)]
        y = forward_image([(gs_ref, k + n) for n in range(3)], hop_t, pair_t, kinds)
        add_pairs(re, im, 3, g_ref[k], y, swap(y))
    for n in range(4):
        acc_ref[2 * n] = re[n]
        acc_ref[2 * n + 1] = im[n]


def outer_side(
    low, win_ref, recv_ref, hop_t, pair_t, us_in, g_in, gs_in, acc_ref,
    us_new, g_ref, gs_new, own, recv, valid,
):
    start = 0 if low else BLK - INNER
    first = -1 if low else SPLIT
    sign = halves((1, LANES))
    edge = [-3, -2, -1] if low else [16, 17, 18]
    e, h = (0, 1) if low else (1, 0)
    for n in range(EDGE):
        elec = recv_ref[pl.ds((e * EDGE + n) * COLS, COLS)]
        hole = recv_ref[pl.ds((h * EDGE + n) * COLS, COLS)]
        us_new[n] = parts_of(elec, hole, sign)
    for k in range(INNER - 4):
        g_ref[start + 2 + k - first] = g_in[k]
    images = [-1, 0, 1] if low else [14, 15, 16]
    kinds_of = {}
    for i in range(-3, 2) if low else range(12, 17):
        kinds_of[i] = (own if 0 <= i < BLK else recv)[0, i % BLK]

    def kind(i, c):
        return jnp.bitwise_and(lax.shift_right_logical(kinds_of[i], 3 * c), 7)

    def us(i):
        return (us_new, edge.index(i)) if i in edge else (us_in, i - start)

    def gs(i):
        return (gs_new, images.index(i)) if i in images else (gs_in, i - start - 2)

    re = [acc_ref[2 * n] for n in range(4)]
    im = [acc_ref[2 * n + 1] for n in range(4)]
    for n, i in enumerate(images):
        kinds = [kind(i - 2, 2), kind(i - 1, 1)] + [kind(i, c) for c in range(4)]
        g = image([us(i - 2 + k) for k in range(5)], hop_t, pair_t, kinds)
        own = 0 <= i < BLK
        if not own:
            g = jnp.where(valid, g, 0.0)
        g_ref[i - first] = g
        gs_new[n] = jnp.concatenate(split3(g), 0)
        if own:
            u = jnp.concatenate([win_ref[e, i - start], win_ref[h, i - start] * sign], 0)
            add_pairs(re, im, 0, u, u, swap(u))
            add_pairs(re, im, 1, u, g, swap(g))
            add_pairs(re, im, 2, g, g, swap(g))
    for i in [0, 1] if low else [12, 13, 14]:
        kinds = [kind(i, c) for c in range(4)]
        y = forward_image([gs(i + k) for k in range(3)], hop_t, pair_t, kinds)
        add_pairs(re, im, 3, g_ref[i - first], y, swap(y))
    if low:
        ref, at = gs(1)
        i, y = -1, product(ref[at], [hop_t[3 * kind(-1, 2)]])
    else:
        i = BLK - 1
        lhs = [ref[at] for ref, at in (gs(i), gs(i + 1))] + [-crossed(gs(i))]
        tabs = [hop_t[3 * kind(i, 0)], hop_t[3 * kind(i, 1)], pair_t[2 * kind(i, 3)]]
        y = product(jnp.concatenate(lhs, 1), tabs)
    add_pairs(re, im, 3, g_ref[i - first], y, swap(y))
    rows = []
    for n in range(4):
        s = 1.0 if n in (0, 2) else -1.0
        w = 2.0 if n == 3 else 1.0
        rows.append(w * sign * (re[n][:COLS] + s * re[n][COLS:]))
        rows.append(w * (im[n][:COLS] - s * im[n][COLS:]))
    return rows


def kinds_row(facts):
    row = facts[0:1] + 8.0 * facts[1:2] + 64.0 * facts[2:3] + 512.0 * facts[3:4]
    return row.astype(jnp.int32)


def outer_kernel(
    win_ref, own_ref, recv_ref, hop_t, pair_t, us_in, g_in, gs_in, acc_ref,
    send_ref, img_ref,
    us_new, g_ref, gs_new,
):
    point, eh, dom = (lax.axis_index(x) for x in ("shift", "eh", "dom"))
    own, recv = kinds_row(own_ref[ROWS:]), kinds_row(recv_ref[ROWS:])
    for side in range(2):

        @pl.when(eh == side)
        def _(side=side):
            rows = outer_side(
                side == 0, win_ref, recv_ref, hop_t, pair_t, us_in, g_in, gs_in, acc_ref,
                us_new, g_ref, gs_new, own, recv, dom > 0 if side == 0 else dom < DOMS - 1,
            )
            for k in range(2):
                total = jnp.concatenate(rows[4 * k : 4 * k + 4], 0).T
                send_ref[k : k + 1] = jnp.sum(total, axis=0, keepdims=True)

    low = eh == 0
    sign = halves((1, LANES))
    facts = jnp.where(recv_ref[ROWS + 6 : ROWS + 7] > 0.5, recv_ref[ROWS:], own_ref[ROWS:])
    four = [facts[4:5, 0:1], facts[4:5, 1:2], facts[5:6, 0:1], facts[5:6, 1:2]]
    params = jnp.concatenate([jnp.broadcast_to(x, (1, COLS)) for x in four], 1)
    send_ref[2:3] = jnp.where(low, params, 0.0)
    send_ref[3:8] = jnp.zeros((5, LANES), F32)
    first = 2 * jnp.bitwise_and(point, 3) + 1
    for k in range(2):
        g = g_ref[first + k]
        elec, hole = g[:COLS], -sign * g[COLS:]
        img_ref[k] = jnp.where(low, elec, hole)
        send_ref[(1 + 4 * k) * 8 : (5 + 4 * k) * 8] = jnp.where(low, hole, elec)


def cmul(a, b):
    return a[0] * b[0] - a[1] * b[1], a[0] * b[1] + a[1] * b[0]


def cadd(a, b):
    return a[0] + b[0], a[1] + b[1]


def cdiv(a, b):
    denom = jnp.maximum(b[0] * b[0] + b[1] * b[1], 1.0)
    scale = 1.0 / denom
    return (a[0] * b[0] + a[1] * b[1]) * scale, (a[1] * b[0] - a[0] * b[1]) * scale


def coefficients(parts):
    sums = jnp.sum(parts[:, : 2 * LANES], axis=0).reshape(4, 2, 1, COLS)
    m0, m1, m2, m3 = ((sums[n, 0], sums[n, 1]) for n in range(4))
    pts = jnp.concatenate([parts[d : d + 1, 2 * LANES :] for d, _ in POINT_AT], 0)
    z, w = ((pts[:, k : k + COLS], pts[:, k + COLS : k + 2 * COLS]) for k in (0, 2 * COLS))

    def minus(a, b):
        return a[0] - b[0], a[1] - b[1]

    def twice(a):
        return 2.0 * a[0], 2.0 * a[1]

    a0 = cdiv(m0, minus(cmul(z, m0), m1))
    az = cmul(a0, z)
    s = (1.0 - az[0], -az[1])
    s2, sa, aa = cmul(s, s), cmul(s, a0), cmul(a0, a0)
    rho = cadd(cadd(cmul(s2, m0), twice(cmul(sa, m1))), cmul(aa, m2))
    c = cadd(s, cdiv(rho, m0))
    cc, ca = cmul(c, c), cmul(c, a0)
    pp = cadd(cadd(cmul(cc, m0), twice(cmul(ca, m1))), cmul(aa, m2))
    php = cadd(cadd(cmul(cc, m1), twice(cmul(ca, m2))), cmul(aa, m3))
    a1 = cdiv(rho, minus(cmul(z, pp), php))
    c0 = cmul(w, cadd(a0, cmul(a1, c)))
    c1 = cmul(w, cmul(a1, a0))
    return jnp.stack([jnp.sum(x, axis=0) for x in (*c0, *c1)])


def combine_kernel(coef_ref, right_ref, img_ref, sent_ref, out_ref):
    sign = -halves((1, LANES))
    point = lax.axis_index("shift")
    holder = (point >= SHIFTS // 2).astype(jnp.int32)
    mine = lax.axis_index("eh") == holder
    for k in range(2):
        b = right_ref[2 * point + k]
        g = jnp.where(mine, img_ref[k], sent_ref[holder, (1 + 4 * k) * 8 : (5 + 4 * k) * 8])
        out = coef_ref[0] * b + coef_ref[1] * (swap(b) * sign)
        out_ref[0, k] = out + coef_ref[2] * g + coef_ref[3] * (swap(g) * sign)


def body(right_side, shifts, quad_weights, hop_table, pair_table, hop_type, pair_type):
    vmem = pl.BlockSpec(memory_space=pltpu.VMEM)
    low = lax.axis_index("eh") == 0
    right = right_side[0]
    inputs = (hop_type.T, pair_type[None], shifts, quad_weights, hop_table, pair_table, right)
    other = lax.ppermute(right, "eh", [(0, 1), (1, 0)])
    facts, hops, pairs, mine = pl.pallas_call(
        fetch_kernel,
        out_shape=[
            jax.ShapeDtypeStruct((8, LANES), F32),
            jax.ShapeDtypeStruct(hop_table.shape, F32),
            jax.ShapeDtypeStruct(pair_table.shape, F32),
            jax.ShapeDtypeStruct(right.shape, F32),
        ],
        in_specs=[pl.BlockSpec(memory_space=pltpu.HBM)] * 7,
        out_specs=[vmem] * 4,
        scratch_shapes=[
            pltpu.VMEM((3, BLK), jnp.int32),
            pltpu.VMEM((1, BLK), jnp.int32),
            pltpu.VMEM((1, 2), F32),
            pltpu.VMEM((1, 2), F32),
            pltpu.SemaphoreType.DMA((7,)),
        ],
        compiler_params=VM,
        name="fetch",
    )(*(pltpu.with_memory_space_constraint(x, pltpu.HBM) for x in inputs))
    at = jnp.where(low, BLK - EDGE, 0)
    edge = [lax.dynamic_slice_in_dim(x, at, EDGE, 0).reshape(-1, LANES) for x in (mine, other)]
    own = jnp.concatenate([*edge, facts], 0)
    own, hops, pairs = lax.optimization_barrier((own, hops, pairs))
    recv = lax.ppermute(own, ALL, halo_pairs())
    hop_t, pair_t = pl.pallas_call(
        tables_kernel,
        out_shape=[
            jax.ShapeDtypeStruct((24, LANES, 3 * LANES), BF16),
            jax.ShapeDtypeStruct((8, LANES, 3 * LANES), BF16),
        ],
        in_specs=[vmem] * 2,
        out_specs=[vmem] * 2,
        compiler_params=VM,
        name="tables",
    )(hops, pairs)
    at = jnp.where(low, 0, BLK - INNER)
    win = jnp.stack([lax.dynamic_slice_in_dim(x, at, INNER, 0) for x in (mine, other)])
    us, g, gs, acc = pl.pallas_call(
        inner_kernel,
        out_shape=[
            jax.ShapeDtypeStruct((INNER, 6 * COLS, LANES), BF16),
            jax.ShapeDtypeStruct((INNER - 4, 2 * COLS, LANES), F32),
            jax.ShapeDtypeStruct((INNER - 4, 6 * COLS, LANES), BF16),
            jax.ShapeDtypeStruct((8, 2 * COLS, LANES), F32),
        ],
        in_specs=[vmem] * 4,
        out_specs=[vmem] * 4,
        scratch_shapes=[
            pltpu.SMEM((8, LANES), F32),
            pltpu.SMEM((INNER, 4), jnp.int32),
            pltpu.SemaphoreType.DMA,
        ],
        compiler_params=VM,
        name="inner",
    )(win, own, hop_t, pair_t)
    send, img = pl.pallas_call(
        outer_kernel,
        out_shape=[
            jax.ShapeDtypeStruct((72, LANES), F32),
            jax.ShapeDtypeStruct((2, COLS, LANES), F32),
        ],
        in_specs=[vmem] * 9,
        out_specs=[vmem] * 2,
        scratch_shapes=[
            pltpu.VMEM((EDGE, 6 * COLS, LANES), BF16),
            pltpu.VMEM((REACH, 2 * COLS, LANES), F32),
            pltpu.VMEM((EDGE, 6 * COLS, LANES), BF16),
        ],
        compiler_params=VM,
        name="outer",
    )(win, own, recv, hop_t, pair_t, us, g, gs, acc)
    sent = lax.all_gather(send, "eh")
    mom = (sent[0, :3] + sent[1, :3]).reshape(1, 1, 3 * LANES)
    mom = jnp.broadcast_to(mom, (DOMS, 1, 3 * LANES))
    parts = lax.all_to_all(mom, "dom", 0, 0)[:, 0]
    coef = coefficients(parts)[:, :, None]
    coef = jnp.broadcast_to(coef, (4, COLS, LANES))
    return pl.pallas_call(
        combine_kernel,
        out_shape=jax.ShapeDtypeStruct((1, 2, COLS, LANES), F32),
        in_specs=[vmem] * 4,
        out_specs=vmem,
        compiler_params=VM,
        name="combine",
    )(coef, mine, img, sent)


def solution(mesh):
    placed = (
        P("eh", "dom", None, None),
        P("shift", None),
        P("shift", None),
        P(),
        P(),
        P("dom", None),
        P("dom"),
    )
    return jax.shard_map(
        body,
        mesh=mesh,
        in_specs=placed,
        out_specs=P("eh", ("dom", "shift"), None, None),
        check_vma=False,
    )
```

```python
import jax
import jax.numpy as jnp
from jax import lax
from jax.experimental import pallas as pl
from jax.experimental.pallas import tpu as pltpu
from jax.sharding import PartitionSpec as P

ALL = ("shift", "dom", "eh")
F32 = jnp.float32
BF16 = jnp.bfloat16
SHIFTS, DOMS, EHS = 8, 32, 2
BLK, COLS, LANES = 16, 32, 128
EDGE = 3
INNER = 11
REACH = 10
SPLIT = 7
ROWS = 2 * EDGE * COLS
VM = pltpu.CompilerParams(vmem_limit_bytes=24 * 1024 * 1024)


def flat(s, d, e):
    return (s * DOMS + d) * EHS + e


TURNS = {(1, 0): 1, (2, 0): 2, (3, 0): 3, (17, 0): 4, (18, 0): 5, (19, 0): 6, (4, 0): 7}
POINT_AT = [(0, 0)] + list(TURNS)


def halo_pairs():
    pairs = []
    for s in range(SHIFTS):
        for d in range(DOMS):
            for e in range(EHS):
                source = d - 1 + 2 * e
                if 0 <= source < DOMS:
                    turn = TURNS.get((d, e), 0)
                    pairs.append((flat(s ^ turn, source, e), flat(s, d, e)))
    return pairs


def halves(shape):
    lane = lax.broadcasted_iota(jnp.int32, shape, len(shape) - 1)
    return jnp.where(lane < LANES // 2, 1.0, -1.0).astype(F32)


def split3(x):
    a = x.astype(BF16)
    r = x - a.astype(F32)
    b = r.astype(BF16)
    c = (r - b.astype(F32)).astype(BF16)
    return a, b, c


def quad(a, b, c, d):
    return jnp.concatenate(
        [jnp.concatenate([a, b], 1), jnp.concatenate([c, d], 1)], 0
    )


def tables_kernel(hop_ref, pair_ref, hop_out, pair_out):
    def put(out, at, mat):
        out[at] = jnp.concatenate(split3(mat), 1)

    for t in range(8):
        re, im = hop_ref[t, 0], hop_ref[t, 1]
        ret, imt = re.T, im.T
        bwd = quad(re, im, -im, re)
        fwd = quad(ret, imt, -imt, ret)
        put(hop_out, 3 * t, fwd)
        put(hop_out, 3 * t + 1, bwd)
        put(hop_out, 3 * t + 2, fwd + bwd)
    for t in range(4):
        re, im = pair_ref[t, 0], pair_ref[t, 1]
        ret, imt = re.T, im.T
        put(pair_out, 2 * t, quad(ret, imt, imt, -ret))
        put(pair_out, 2 * t + 1, quad(-re, im, im, re))


def product(lhs, tabs):
    rows = lhs.shape[0] // 3
    both = jnp.concatenate([t[:, : 2 * LANES] for t in tabs], 0)
    third = jnp.concatenate([t[:, 2 * LANES :] for t in tabs], 0)
    big = jnp.dot(lhs, both, preferred_element_type=F32)
    small = jnp.dot(lhs[:rows], third, preferred_element_type=F32)
    small = small + big[2 * rows :, :LANES] + big[rows : 2 * rows, LANES:]
    small = small + (big[:rows, LANES:] + big[rows : 2 * rows, :LANES])
    return big[:rows, :LANES] + small


def crossed(block):
    ref, at = block
    zero = jnp.zeros((COLS, LANES), BF16)
    rows = []
    for part in range(3):
        rows += [ref[at, pl.ds((2 * part + 1) * COLS, COLS)], zero]
    return jnp.concatenate(rows, 0)


def crossed_up(block):
    ref, at = block
    zero = jnp.zeros((COLS, LANES), BF16)
    rows = []
    for part in range(3):
        rows += [zero, ref[at, pl.ds(2 * part * COLS, COLS)]]
    return jnp.concatenate(rows, 0)


def image(blocks, hop_t, pair_t, kinds):
    back2, back1, here, on1, on2, pair = kinds
    lhs = [ref[at] for ref, at in blocks]
    lhs += [crossed(blocks[2]), crossed_up(blocks[2])]
    tabs = [hop_t[3 * back2 + 1], hop_t[3 * back1 + 1], hop_t[3 * here + 2]]
    tabs += [hop_t[3 * on1], hop_t[3 * on2], pair_t[2 * pair], pair_t[2 * pair + 1]]
    return product(jnp.concatenate(lhs, 1), tabs)


def forward_image(blocks, hop_t, pair_t, kinds):
    here, on1, on2, pair = kinds
    lhs = [ref[at] for ref, at in blocks] + [-crossed(blocks[0])]
    tabs = [hop_t[3 * here], hop_t[3 * on1], hop_t[3 * on2], pair_t[2 * pair]]
    return product(jnp.concatenate(lhs, 1), tabs)


def swap(x):
    return pltpu.roll(x, LANES // 2, 1)


def add_pairs(re, im, n, a, b, b_swapped):
    re[n] = a * b if re[n] is None else re[n] + a * b
    im[n] = a * b_swapped if im[n] is None else im[n] + a * b_swapped


def fetch_kernel(
    hop_s, pair_s, shift_ref, weight_ref, hop_ref, pair_ref, right_ref,
    facts_ref, hop_v, pair_v, mine_ref,
    hop_k, pair_k, shift_v, weight_v, sem,
):
    copies = [
        pltpu.make_async_copy(source, to, sem.at[n])
        for n, (source, to) in enumerate(
            (
                (hop_s, hop_k),
                (pair_s, pair_k),
                (shift_ref, shift_v),
                (weight_ref, weight_v),
                (hop_ref, hop_v),
                (pair_ref, pair_v),
                (right_ref, mine_ref),
            )
        )
    ]
    for c in copies:
        c.start()
    facts_ref[...] = jnp.zeros_like(facts_ref)
    facts_ref[6:7] = jnp.ones((1, LANES), F32)
    for c in copies:
        c.wait()
    facts_ref[0:3, :BLK] = hop_k[...].astype(F32)
    facts_ref[3:4, :BLK] = pair_k[...].astype(F32)
    facts_ref[4:5, :2] = shift_v[...]
    facts_ref[5:6, :2] = weight_v[...]


def parts_of(elec, hole, sign):
    return jnp.concatenate(split3(jnp.concatenate([elec, hole * sign], 0)), 0)


def inner_kernel(
    win_ref, own_ref, hop_t, pair_t,
    us_ref, g_ref, gs_ref, acc_ref,
    own_s, kind_s, sem,
):
    facts = pltpu.make_async_copy(own_ref.at[pl.ds(ROWS, 8)], own_s, sem)
    facts.start()
    low = lax.axis_index("eh") == 0
    sign = halves((1, LANES))

    def both(a):
        x, y = win_ref[0, a], win_ref[1, a]
        return jnp.where(low, x, y), jnp.where(low, y, x)

    for a in range(INNER):
        us_ref[a] = parts_of(*both(a), sign)
    facts.wait()
    for a in range(INNER - 2):
        for c in range(4):
            kind_s[a, c] = jnp.where(low, own_s[c, a], own_s[c, BLK - INNER + a]).astype(jnp.int32)
    re, im = [None] * 4, [None] * 4
    for k in range(INNER - 4):
        kinds = [kind_s[k, 2], kind_s[k + 1, 1]] + [kind_s[k + 2, c] for c in range(4)]
        g = image([(us_ref, k + n) for n in range(5)], hop_t, pair_t, kinds)
        g_ref[k] = g
        gs_ref[k] = jnp.concatenate(split3(g), 0)
        elec, hole = both(k + 2)
        u = jnp.concatenate([elec, hole * sign], 0)
        if k + 2 >= SPLIT:
            u, g = jnp.where(low, 0.0, u), jnp.where(low, 0.0, g)
        add_pairs(re, im, 0, u, u, swap(u))
        add_pairs(re, im, 1, u, g, swap(g))
        add_pairs(re, im, 2, g, g, swap(g))
    for k in range(INNER - 6):
        kinds = [kind_s[k + 2, c] for c in range(4)]
        y = forward_image([(gs_ref, k + n) for n in range(3)], hop_t, pair_t, kinds)
        add_pairs(re, im, 3, g_ref[k], y, swap(y))
    for n in range(4):
        acc_ref[2 * n] = re[n]
        acc_ref[2 * n + 1] = im[n]


def outer_side(
    low, win_ref, recv_ref, hop_t, pair_t, us_in, g_in, gs_in, acc_ref,
    us_new, g_ref, gs_new, own, recv, valid,
):
    start = 0 if low else BLK - INNER
    first = -1 if low else SPLIT
    sign = halves((1, LANES))
    edge = [-3, -2, -1] if low else [16, 17, 18]
    e, h = (0, 1) if low else (1, 0)
    for n in range(EDGE):
        elec = recv_ref[pl.ds((e * EDGE + n) * COLS, COLS)]
        hole = recv_ref[pl.ds((h * EDGE + n) * COLS, COLS)]
        us_new[n] = parts_of(elec, hole, sign)
    for k in range(INNER - 4):
        g_ref[start + 2 + k - first] = g_in[k]
    images = [-1, 0, 1] if low else [14, 15, 16]
    kinds_of = {}
    for i in range(-3, 2) if low else range(12, 17):
        kinds_of[i] = (own if 0 <= i < BLK else recv)[0, i % BLK]

    def kind(i, c):
        return jnp.bitwise_and(lax.shift_right_logical(kinds_of[i], 3 * c), 7)

    def us(i):
        return (us_new, edge.index(i)) if i in edge else (us_in, i - start)

    def gs(i):
        return (gs_new, images.index(i)) if i in images else (gs_in, i - start - 2)

    re = [acc_ref[2 * n] for n in range(4)]
    im = [acc_ref[2 * n + 1] for n in range(4)]
    for n, i in enumerate(images):
        kinds = [kind(i - 2, 2), kind(i - 1, 1)] + [kind(i, c) for c in range(4)]
        g = image([us(i - 2 + k) for k in range(5)], hop_t, pair_t, kinds)
        own = 0 <= i < BLK
        if not own:
            g = jnp.where(valid, g, 0.0)
        g_ref[i - first] = g
        gs_new[n] = jnp.concatenate(split3(g), 0)
        if own:
            u = jnp.concatenate([win_ref[e, i - start], win_ref[h, i - start] * sign], 0)
            add_pairs(re, im, 0, u, u, swap(u))
            add_pairs(re, im, 1, u, g, swap(g))
            add_pairs(re, im, 2, g, g, swap(g))
    for i in [0, 1] if low else [12, 13, 14]:
        kinds = [kind(i, c) for c in range(4)]
        y = forward_image([gs(i + k) for k in range(3)], hop_t, pair_t, kinds)
        add_pairs(re, im, 3, g_ref[i - first], y, swap(y))
    if low:
        ref, at = gs(1)
        i, y = -1, product(ref[at], [hop_t[3 * kind(-1, 2)]])
    else:
        i = BLK - 1
        lhs = [ref[at] for ref, at in (gs(i), gs(i + 1))] + [-crossed(gs(i))]
        tabs = [hop_t[3 * kind(i, 0)], hop_t[3 * kind(i, 1)], pair_t[2 * kind(i, 3)]]
        y = product(jnp.concatenate(lhs, 1), tabs)
    add_pairs(re, im, 3, g_ref[i - first], y, swap(y))
    rows = []
    for n in range(4):
        s = 1.0 if n in (0, 2) else -1.0
        w = 2.0 if n == 3 else 1.0
        rows.append(w * sign * (re[n][:COLS] + s * re[n][COLS:]))
        rows.append(w * (im[n][:COLS] - s * im[n][COLS:]))
    return rows


def kinds_row(facts):
    row = facts[0:1] + 8.0 * facts[1:2] + 64.0 * facts[2:3] + 512.0 * facts[3:4]
    return row.astype(jnp.int32)


def outer_kernel(
    win_ref, own_ref, recv_ref, hop_t, pair_t, us_in, g_in, gs_in, acc_ref,
    send_ref, img_ref,
    us_new, g_ref, gs_new,
):
    point, eh, dom = (lax.axis_index(x) for x in ("shift", "eh", "dom"))
    own, recv = kinds_row(own_ref[ROWS:]), kinds_row(recv_ref[ROWS:])
    for side in range(2):

        @pl.when(eh == side)
        def _(side=side):
            rows = outer_side(
                side == 0, win_ref, recv_ref, hop_t, pair_t, us_in, g_in, gs_in, acc_ref,
                us_new, g_ref, gs_new, own, recv, dom > 0 if side == 0 else dom < DOMS - 1,
            )
            for k in range(2):
                total = jnp.concatenate(rows[4 * k : 4 * k + 4], 0).T
                send_ref[k : k + 1] = jnp.sum(total, axis=0, keepdims=True)

    low = eh == 0
    sign = halves((1, LANES))
    facts = jnp.where(recv_ref[ROWS + 6 : ROWS + 7] > 0.5, recv_ref[ROWS:], own_ref[ROWS:])
    four = [facts[4:5, 0:1], facts[4:5, 1:2], facts[5:6, 0:1], facts[5:6, 1:2]]
    params = jnp.concatenate([jnp.broadcast_to(x, (1, COLS)) for x in four], 1)
    send_ref[2:3] = jnp.where(low, params, 0.0)
    send_ref[3:8] = jnp.zeros((5, LANES), F32)
    first = 2 * jnp.bitwise_and(point, 3) + 1
    for k in range(2):
        g = g_ref[first + k]
        elec, hole = g[:COLS], -sign * g[COLS:]
        img_ref[k] = jnp.where(low, elec, hole)
        send_ref[(1 + 4 * k) * 8 : (5 + 4 * k) * 8] = jnp.where(low, hole, elec)


def cmul(a, b):
    return a[0] * b[0] - a[1] * b[1], a[0] * b[1] + a[1] * b[0]


def cadd(a, b):
    return a[0] + b[0], a[1] + b[1]


def cdiv(a, b):
    denom = jnp.maximum(b[0] * b[0] + b[1] * b[1], 1.0)
    scale = 1.0 / denom
    return (a[0] * b[0] + a[1] * b[1]) * scale, (a[1] * b[0] - a[0] * b[1]) * scale


def coefficients(parts):
    sums = jnp.sum(parts[:, : 2 * LANES], axis=0, keepdims=True)
    sums = [sums[:, k * COLS : (k + 1) * COLS] for k in range(8)]
    m0, m1, m2, m3 = zip(sums[::2], sums[1::2])
    pts = jnp.concatenate([parts[d : d + 1, 2 * LANES :] for d, _ in POINT_AT], 0)
    z, w = ((pts[:, k : k + COLS], pts[:, k + COLS : k + 2 * COLS]) for k in (0, 2 * COLS))

    def minus(a, b):
        return a[0] - b[0], a[1] - b[1]

    def twice(a):
        return 2.0 * a[0], 2.0 * a[1]

    a0 = cdiv(m0, minus(cmul(z, m0), m1))
    az = cmul(a0, z)
    s = (1.0 - az[0], -az[1])
    s2, sa, aa = cmul(s, s), cmul(s, a0), cmul(a0, a0)
    rho = cadd(cadd(cmul(s2, m0), twice(cmul(sa, m1))), cmul(aa, m2))
    c = cadd(s, cdiv(rho, m0))
    cc, ca = cmul(c, c), cmul(c, a0)
    pp = cadd(cadd(cmul(cc, m0), twice(cmul(ca, m1))), cmul(aa, m2))
    php = cadd(cadd(cmul(cc, m1), twice(cmul(ca, m2))), cmul(aa, m3))
    a1 = cdiv(rho, minus(cmul(z, pp), php))
    c0 = cmul(w, cadd(a0, cmul(a1, c)))
    c1 = cmul(w, cmul(a1, a0))
    return jnp.stack([jnp.sum(x, axis=0) for x in (*c0, *c1)])


def combine_kernel(coef_ref, right_ref, img_ref, sent_ref, out_ref):
    sign = -halves((1, LANES))
    point = lax.axis_index("shift")
    holder = (point >= SHIFTS // 2).astype(jnp.int32)
    mine = lax.axis_index("eh") == holder
    for k in range(2):
        b = right_ref[2 * point + k]
        g = jnp.where(mine, img_ref[k], sent_ref[holder, (1 + 4 * k) * 8 : (5 + 4 * k) * 8])
        out = coef_ref[0] * b + coef_ref[1] * (swap(b) * sign)
        out_ref[0, k] = out + coef_ref[2] * g + coef_ref[3] * (swap(g) * sign)


def body(right_side, shifts, quad_weights, hop_table, pair_table, hop_type, pair_type):
    vmem = pl.BlockSpec(memory_space=pltpu.VMEM)
    low = lax.axis_index("eh") == 0
    right = right_side[0]
    inputs = (hop_type.T, pair_type[None], shifts, quad_weights, hop_table, pair_table, right)
    other = lax.ppermute(right, "eh", [(0, 1), (1, 0)])
    facts, hops, pairs, mine = pl.pallas_call(
        fetch_kernel,
        out_shape=[
            jax.ShapeDtypeStruct((8, LANES), F32),
            jax.ShapeDtypeStruct(hop_table.shape, F32),
            jax.ShapeDtypeStruct(pair_table.shape, F32),
            jax.ShapeDtypeStruct(right.shape, F32),
        ],
        in_specs=[pl.BlockSpec(memory_space=pltpu.HBM)] * 7,
        out_specs=[vmem] * 4,
        scratch_shapes=[
            pltpu.VMEM((3, BLK), jnp.int32),
            pltpu.VMEM((1, BLK), jnp.int32),
            pltpu.VMEM((1, 2), F32),
            pltpu.VMEM((1, 2), F32),
            pltpu.SemaphoreType.DMA((7,)),
        ],
        compiler_params=VM,
        name="fetch",
    )(*(pltpu.with_memory_space_constraint(x, pltpu.HBM) for x in inputs))
    at = jnp.where(low, BLK - EDGE, 0)
    edge = [lax.dynamic_slice_in_dim(x, at, EDGE, 0).reshape(-1, LANES) for x in (mine, other)]
    own = jnp.concatenate([*edge, facts], 0)
    own, hops, pairs = lax.optimization_barrier((own, hops, pairs))
    recv = lax.ppermute(own, ALL, halo_pairs())
    hop_t, pair_t = pl.pallas_call(
        tables_kernel,
        out_shape=[
            jax.ShapeDtypeStruct((24, LANES, 3 * LANES), BF16),
            jax.ShapeDtypeStruct((8, LANES, 3 * LANES), BF16),
        ],
        in_specs=[vmem] * 2,
        out_specs=[vmem] * 2,
        compiler_params=VM,
        name="tables",
    )(hops, pairs)
    at = jnp.where(low, 0, BLK - INNER)
    win = jnp.stack([lax.dynamic_slice_in_dim(x, at, INNER, 0) for x in (mine, other)])
    us, g, gs, acc = pl.pallas_call(
        inner_kernel,
        out_shape=[
            jax.ShapeDtypeStruct((INNER, 6 * COLS, LANES), BF16),
            jax.ShapeDtypeStruct((INNER - 4, 2 * COLS, LANES), F32),
            jax.ShapeDtypeStruct((INNER - 4, 6 * COLS, LANES), BF16),
            jax.ShapeDtypeStruct((8, 2 * COLS, LANES), F32),
        ],
        in_specs=[vmem] * 4,
        out_specs=[vmem] * 4,
        scratch_shapes=[
            pltpu.SMEM((8, LANES), F32),
            pltpu.SMEM((INNER, 4), jnp.int32),
            pltpu.SemaphoreType.DMA,
        ],
        compiler_params=VM,
        name="inner",
    )(win, own, hop_t, pair_t)
    send, img = pl.pallas_call(
        outer_kernel,
        out_shape=[
            jax.ShapeDtypeStruct((72, LANES), F32),
            jax.ShapeDtypeStruct((2, COLS, LANES), F32),
        ],
        in_specs=[vmem] * 9,
        out_specs=[vmem] * 2,
        scratch_shapes=[
            pltpu.VMEM((EDGE, 6 * COLS, LANES), BF16),
            pltpu.VMEM((REACH, 2 * COLS, LANES), F32),
            pltpu.VMEM((EDGE, 6 * COLS, LANES), BF16),
        ],
        compiler_params=VM,
        name="outer",
    )(win, own, recv, hop_t, pair_t, us, g, gs, acc)
    sent = lax.all_gather(send, "eh")
    mom = (sent[0, :3] + sent[1, :3]).reshape(1, 1, 3 * LANES)
    mom = jnp.broadcast_to(mom, (DOMS, 1, 3 * LANES))
    parts = lax.all_to_all(mom, "dom", 0, 0)[:, 0]
    coef = coefficients(parts)[:, :, None]
    coef = jnp.broadcast_to(coef, (4, COLS, LANES))
    return pl.pallas_call(
        combine_kernel,
        out_shape=jax.ShapeDtypeStruct((1, 2, COLS, LANES), F32),
        in_specs=[vmem] * 4,
        out_specs=vmem,
        compiler_params=VM,
        name="combine",
    )(coef, mine, img, sent)


def solution(mesh):
    placed = (
        P("eh", "dom", None, None),
        P("shift", None),
        P("shift", None),
        P(),
        P(),
        P("dom", None),
        P("dom"),
    )
    return jax.shard_map(
        body,
        mesh=mesh,
        in_specs=placed,
        out_specs=P("eh", ("dom", "shift"), None, None),
        check_vma=False,
    )
```

```python
import jax
import jax.numpy as jnp
from jax import lax
from jax.experimental import pallas as pl
from jax.experimental.pallas import tpu as pltpu
from jax.sharding import PartitionSpec as P

ALL = ("shift", "dom", "eh")
F32 = jnp.float32
BF16 = jnp.bfloat16
SHIFTS, DOMS, EHS = 8, 32, 2
BLK, COLS, LANES = 16, 32, 128
EDGE = 3
INNER = 11
REACH = 10
SPLIT = 7
ROWS = 2 * EDGE * COLS
VM = pltpu.CompilerParams(vmem_limit_bytes=24 * 1024 * 1024)


def flat(s, d, e):
    return (s * DOMS + d) * EHS + e


TURNS = {(1, 0): 1, (2, 0): 2, (3, 0): 3, (17, 0): 4, (18, 0): 5, (19, 0): 6, (4, 0): 7}
POINT_AT = [(0, 0)] + list(TURNS)


def halo_pairs():
    pairs = []
    for s in range(SHIFTS):
        for d in range(DOMS):
            for e in range(EHS):
                source = d - 1 + 2 * e
                if 0 <= source < DOMS:
                    turn = TURNS.get((d, e), 0)
                    pairs.append((flat(s ^ turn, source, e), flat(s, d, e)))
    return pairs


def halves(shape):
    lane = lax.broadcasted_iota(jnp.int32, shape, len(shape) - 1)
    return jnp.where(lane < LANES // 2, 1.0, -1.0).astype(F32)


def split3(x):
    a = x.astype(BF16)
    r = x - a.astype(F32)
    b = r.astype(BF16)
    c = (r - b.astype(F32)).astype(BF16)
    return a, b, c


def quad(a, b, c, d):
    return jnp.concatenate(
        [jnp.concatenate([a, b], 1), jnp.concatenate([c, d], 1)], 0
    )


def tables_kernel(hop_ref, pair_ref, hop_out, pair_out):
    def put(out, at, mat):
        out[at] = jnp.concatenate(split3(mat), 1)

    for t in range(8):
        re, im = hop_ref[t, 0], hop_ref[t, 1]
        ret, imt = re.T, im.T
        bwd = quad(re, im, -im, re)
        fwd = quad(ret, imt, -imt, ret)
        put(hop_out, 3 * t, fwd)
        put(hop_out, 3 * t + 1, bwd)
        put(hop_out, 3 * t + 2, fwd + bwd)
    for t in range(4):
        re, im = pair_ref[t, 0], pair_ref[t, 1]
        ret, imt = re.T, im.T
        put(pair_out, 2 * t, quad(ret, imt, imt, -ret))
        put(pair_out, 2 * t + 1, quad(-re, im, im, re))


def product(lhs, tabs):
    rows = lhs.shape[0] // 3
    both = jnp.concatenate([t[:, : 2 * LANES] for t in tabs], 0)
    third = jnp.concatenate([t[:, 2 * LANES :] for t in tabs], 0)
    big = jnp.dot(lhs, both, preferred_element_type=F32)
    small = jnp.dot(lhs[:rows], third, preferred_element_type=F32)
    small = small + big[2 * rows :, :LANES] + big[rows : 2 * rows, LANES:]
    small = small + (big[:rows, LANES:] + big[rows : 2 * rows, :LANES])
    return big[:rows, :LANES] + small


def crossed(block):
    ref, at = block
    zero = jnp.zeros((COLS, LANES), BF16)
    rows = []
    for part in range(3):
        rows += [ref[at, pl.ds((2 * part + 1) * COLS, COLS)], zero]
    return jnp.concatenate(rows, 0)


def crossed_up(block):
    ref, at = block
    zero = jnp.zeros((COLS, LANES), BF16)
    rows = []
    for part in range(3):
        rows += [zero, ref[at, pl.ds(2 * part * COLS, COLS)]]
    return jnp.concatenate(rows, 0)


def image(blocks, hop_t, pair_t, kinds):
    back2, back1, here, on1, on2, pair = kinds
    lhs = [ref[at] for ref, at in blocks]
    lhs += [crossed(blocks[2]), crossed_up(blocks[2])]
    tabs = [hop_t[3 * back2 + 1], hop_t[3 * back1 + 1], hop_t[3 * here + 2]]
    tabs += [hop_t[3 * on1], hop_t[3 * on2], pair_t[2 * pair], pair_t[2 * pair + 1]]
    return product(jnp.concatenate(lhs, 1), tabs)


def forward_image(blocks, hop_t, pair_t, kinds):
    here, on1, on2, pair = kinds
    lhs = [ref[at] for ref, at in blocks] + [-crossed(blocks[0])]
    tabs = [hop_t[3 * here], hop_t[3 * on1], hop_t[3 * on2], pair_t[2 * pair]]
    return product(jnp.concatenate(lhs, 1), tabs)


def swap(x):
    return pltpu.roll(x, LANES // 2, 1)


def add_pairs(re, im, n, a, b, b_swapped):
    re[n] = a * b if re[n] is None else re[n] + a * b
    im[n] = a * b_swapped if im[n] is None else im[n] + a * b_swapped


def fetch_kernel(
    hop_s, pair_s, shift_ref, weight_ref, hop_ref, pair_ref, right_ref,
    facts_ref, hop_v, pair_v, mine_ref,
    hop_k, pair_k, shift_v, weight_v, sem,
):
    copies = [
        pltpu.make_async_copy(source, to, sem.at[n])
        for n, (source, to) in enumerate(
            (
                (hop_s, hop_k),
                (pair_s, pair_k),
                (shift_ref, shift_v),
                (weight_ref, weight_v),
                (hop_ref, hop_v),
                (pair_ref, pair_v),
                (right_ref, mine_ref),
            )
        )
    ]
    for c in copies:
        c.start()
    facts_ref[...] = jnp.zeros_like(facts_ref)
    facts_ref[6:7] = jnp.ones((1, LANES), F32)
    for c in copies:
        c.wait()
    facts_ref[0:3, :BLK] = hop_k[...].astype(F32)
    facts_ref[3:4, :BLK] = pair_k[...].astype(F32)
    facts_ref[4:5, :2] = shift_v[...]
    facts_ref[5:6, :2] = weight_v[...]


def parts_of(elec, hole, sign):
    return jnp.concatenate(split3(jnp.concatenate([elec, hole * sign], 0)), 0)


def inner_kernel(
    win_ref, own_ref, hop_t, pair_t,
    us_ref, g_ref, gs_ref, acc_ref,
):
    low = lax.axis_index("eh") == 0
    own = kinds_row(own_ref[ROWS:])
    own = [jnp.where(low, own[0, a], own[0, BLK - INNER + a]) for a in range(INNER - 2)]

    def kind(a, c):
        return jnp.bitwise_and(lax.shift_right_logical(own[a], 3 * c), 7)

    sign = halves((1, LANES))

    def both(a):
        x, y = win_ref[0, a], win_ref[1, a]
        return jnp.where(low, x, y), jnp.where(low, y, x)

    for a in range(INNER):
        us_ref[a] = parts_of(*both(a), sign)
    re, im = [None] * 4, [None] * 4
    for k in range(INNER - 4):
        kinds = [kind(k, 2), kind(k + 1, 1)] + [kind(k + 2, c) for c in range(4)]
        g = image([(us_ref, k + n) for n in range(5)], hop_t, pair_t, kinds)
        g_ref[k] = g
        gs_ref[k] = jnp.concatenate(split3(g), 0)
        elec, hole = both(k + 2)
        u = jnp.concatenate([elec, hole * sign], 0)
        if k + 2 >= SPLIT:
            u, g = jnp.where(low, 0.0, u), jnp.where(low, 0.0, g)
        add_pairs(re, im, 0, u, u, swap(u))
        add_pairs(re, im, 1, u, g, swap(g))
        add_pairs(re, im, 2, g, g, swap(g))
    for k in range(INNER - 6):
        kinds = [kind(k + 2, c) for c in range(4)]
        y = forward_image([(gs_ref, k + n) for n in range(3)], hop_t, pair_t, kinds)
        add_pairs(re, im, 3, g_ref[k], y, swap(y))
    for n in range(4):
        acc_ref[2 * n] = re[n]
        acc_ref[2 * n + 1] = im[n]


def outer_side(
    low, win_ref, recv_ref, hop_t, pair_t, us_in, g_in, gs_in, acc_ref,
    us_new, g_ref, gs_new, own, recv, valid,
):
    start = 0 if low else BLK - INNER
    first = -1 if low else SPLIT
    sign = halves((1, LANES))
    edge = [-3, -2, -1] if low else [16, 17, 18]
    e, h = (0, 1) if low else (1, 0)
    for n in range(EDGE):
        elec = recv_ref[pl.ds((e * EDGE + n) * COLS, COLS)]
        hole = recv_ref[pl.ds((h * EDGE + n) * COLS, COLS)]
        us_new[n] = parts_of(elec, hole, sign)
    for k in range(INNER - 4):
        g_ref[start + 2 + k - first] = g_in[k]
    images = [-1, 0, 1] if low else [14, 15, 16]
    kinds_of = {}
    for i in range(-3, 2) if low else range(12, 17):
        kinds_of[i] = (own if 0 <= i < BLK else recv)[0, i % BLK]

    def kind(i, c):
        return jnp.bitwise_and(lax.shift_right_logical(kinds_of[i], 3 * c), 7)

    def us(i):
        return (us_new, edge.index(i)) if i in edge else (us_in, i - start)

    def gs(i):
        return (gs_new, images.index(i)) if i in images else (gs_in, i - start - 2)

    re = [acc_ref[2 * n] for n in range(4)]
    im = [acc_ref[2 * n + 1] for n in range(4)]
    for n, i in enumerate(images):
        kinds = [kind(i - 2, 2), kind(i - 1, 1)] + [kind(i, c) for c in range(4)]
        g = image([us(i - 2 + k) for k in range(5)], hop_t, pair_t, kinds)
        own = 0 <= i < BLK
        if not own:
            g = jnp.where(valid, g, 0.0)
        g_ref[i - first] = g
        gs_new[n] = jnp.concatenate(split3(g), 0)
        if own:
            u = jnp.concatenate([win_ref[e, i - start], win_ref[h, i - start] * sign], 0)
            add_pairs(re, im, 0, u, u, swap(u))
            add_pairs(re, im, 1, u, g, swap(g))
            add_pairs(re, im, 2, g, g, swap(g))
    for i in [0, 1] if low else [12, 13, 14]:
        kinds = [kind(i, c) for c in range(4)]
        y = forward_image([gs(i + k) for k in range(3)], hop_t, pair_t, kinds)
        add_pairs(re, im, 3, g_ref[i - first], y, swap(y))
    if low:
        ref, at = gs(1)
        i, y = -1, product(ref[at], [hop_t[3 * kind(-1, 2)]])
    else:
        i = BLK - 1
        lhs = [ref[at] for ref, at in (gs(i), gs(i + 1))] + [-crossed(gs(i))]
        tabs = [hop_t[3 * kind(i, 0)], hop_t[3 * kind(i, 1)], pair_t[2 * kind(i, 3)]]
        y = product(jnp.concatenate(lhs, 1), tabs)
    add_pairs(re, im, 3, g_ref[i - first], y, swap(y))
    rows = []
    for n in range(4):
        s = 1.0 if n in (0, 2) else -1.0
        w = 2.0 if n == 3 else 1.0
        rows.append(w * sign * (re[n][:COLS] + s * re[n][COLS:]))
        rows.append(w * (im[n][:COLS] - s * im[n][COLS:]))
    return rows


def kinds_row(facts):
    row = facts[0:1] + 8.0 * facts[1:2] + 64.0 * facts[2:3] + 512.0 * facts[3:4]
    return row.astype(jnp.int32)


def outer_kernel(
    win_ref, own_ref, recv_ref, hop_t, pair_t, us_in, g_in, gs_in, acc_ref,
    send_ref, img_ref,
    us_new, g_ref, gs_new,
):
    point, eh, dom = (lax.axis_index(x) for x in ("shift", "eh", "dom"))
    own, recv = kinds_row(own_ref[ROWS:]), kinds_row(recv_ref[ROWS:])
    for side in range(2):

        @pl.when(eh == side)
        def _(side=side):
            rows = outer_side(
                side == 0, win_ref, recv_ref, hop_t, pair_t, us_in, g_in, gs_in, acc_ref,
                us_new, g_ref, gs_new, own, recv, dom > 0 if side == 0 else dom < DOMS - 1,
            )
            for k in range(2):
                total = jnp.concatenate(rows[4 * k : 4 * k + 4], 0).T
                send_ref[k : k + 1] = jnp.sum(total, axis=0, keepdims=True)

    low = eh == 0
    sign = halves((1, LANES))
    facts = jnp.where(recv_ref[ROWS + 6 : ROWS + 7] > 0.5, recv_ref[ROWS:], own_ref[ROWS:])
    four = [facts[4:5, 0:1], facts[4:5, 1:2], facts[5:6, 0:1], facts[5:6, 1:2]]
    params = jnp.concatenate([jnp.broadcast_to(x, (1, COLS)) for x in four], 1)
    send_ref[2:3] = jnp.where(low, params, 0.0)
    send_ref[3:8] = jnp.zeros((5, LANES), F32)
    first = 2 * jnp.bitwise_and(point, 3) + 1
    for k in range(2):
        g = g_ref[first + k]
        elec, hole = g[:COLS], -sign * g[COLS:]
        img_ref[k] = jnp.where(low, elec, hole)
        send_ref[(1 + 4 * k) * 8 : (5 + 4 * k) * 8] = jnp.where(low, hole, elec)


def cmul(a, b):
    return a[0] * b[0] - a[1] * b[1], a[0] * b[1] + a[1] * b[0]


def cadd(a, b):
    return a[0] + b[0], a[1] + b[1]


def cdiv(a, b):
    denom = jnp.maximum(b[0] * b[0] + b[1] * b[1], 1.0)
    scale = 1.0 / denom
    return (a[0] * b[0] + a[1] * b[1]) * scale, (a[1] * b[0] - a[0] * b[1]) * scale


def coefficients(parts):
    sums = jnp.sum(parts[:, : 2 * LANES], axis=0).reshape(4, 2, 1, COLS)
    m0, m1, m2, m3 = ((sums[n, 0], sums[n, 1]) for n in range(4))
    pts = jnp.concatenate([parts[d : d + 1, 2 * LANES :] for d, _ in POINT_AT], 0)
    z, w = ((pts[:, k : k + COLS], pts[:, k + COLS : k + 2 * COLS]) for k in (0, 2 * COLS))

    def minus(a, b):
        return a[0] - b[0], a[1] - b[1]

    def twice(a):
        return 2.0 * a[0], 2.0 * a[1]

    a0 = cdiv(m0, minus(cmul(z, m0), m1))
    az = cmul(a0, z)
    s = (1.0 - az[0], -az[1])
    s2, sa, aa = cmul(s, s), cmul(s, a0), cmul(a0, a0)
    rho = cadd(cadd(cmul(s2, m0), twice(cmul(sa, m1))), cmul(aa, m2))
    c = cadd(s, cdiv(rho, m0))
    cc, ca = cmul(c, c), cmul(c, a0)
    pp = cadd(cadd(cmul(cc, m0), twice(cmul(ca, m1))), cmul(aa, m2))
    php = cadd(cadd(cmul(cc, m1), twice(cmul(ca, m2))), cmul(aa, m3))
    a1 = cdiv(rho, minus(cmul(z, pp), php))
    c0 = cmul(w, cadd(a0, cmul(a1, c)))
    c1 = cmul(w, cmul(a1, a0))
    return jnp.stack([jnp.sum(x, axis=0) for x in (*c0, *c1)])


def combine_kernel(coef_ref, right_ref, img_ref, sent_ref, out_ref):
    sign = -halves((1, LANES))
    point = lax.axis_index("shift")
    holder = (point >= SHIFTS // 2).astype(jnp.int32)
    mine = lax.axis_index("eh") == holder
    for k in range(2):
        b = right_ref[2 * point + k]
        g = jnp.where(mine, img_ref[k], sent_ref[holder, (1 + 4 * k) * 8 : (5 + 4 * k) * 8])
        out = coef_ref[0] * b + coef_ref[1] * (swap(b) * sign)
        out_ref[0, k] = out + coef_ref[2] * g + coef_ref[3] * (swap(g) * sign)


def body(right_side, shifts, quad_weights, hop_table, pair_table, hop_type, pair_type):
    vmem = pl.BlockSpec(memory_space=pltpu.VMEM)
    low = lax.axis_index("eh") == 0
    right = right_side[0]
    inputs = (hop_type.T, pair_type[None], shifts, quad_weights, hop_table, pair_table, right)
    other = lax.ppermute(right, "eh", [(0, 1), (1, 0)])
    facts, hops, pairs, mine = pl.pallas_call(
        fetch_kernel,
        out_shape=[
            jax.ShapeDtypeStruct((8, LANES), F32),
            jax.ShapeDtypeStruct(hop_table.shape, F32),
            jax.ShapeDtypeStruct(pair_table.shape, F32),
            jax.ShapeDtypeStruct(right.shape, F32),
        ],
        in_specs=[pl.BlockSpec(memory_space=pltpu.HBM)] * 7,
        out_specs=[vmem] * 4,
        scratch_shapes=[
            pltpu.VMEM((3, BLK), jnp.int32),
            pltpu.VMEM((1, BLK), jnp.int32),
            pltpu.VMEM((1, 2), F32),
            pltpu.VMEM((1, 2), F32),
            pltpu.SemaphoreType.DMA((7,)),
        ],
        compiler_params=VM,
        name="fetch",
    )(*(pltpu.with_memory_space_constraint(x, pltpu.HBM) for x in inputs))
    at = jnp.where(low, BLK - EDGE, 0)
    edge = [lax.dynamic_slice_in_dim(x, at, EDGE, 0).reshape(-1, LANES) for x in (mine, other)]
    own = jnp.concatenate([*edge, facts], 0)
    own, hops, pairs = lax.optimization_barrier((own, hops, pairs))
    recv = lax.ppermute(own, ALL, halo_pairs())
    hop_t, pair_t = pl.pallas_call(
        tables_kernel,
        out_shape=[
            jax.ShapeDtypeStruct((24, LANES, 3 * LANES), BF16),
            jax.ShapeDtypeStruct((8, LANES, 3 * LANES), BF16),
        ],
        in_specs=[vmem] * 2,
        out_specs=[vmem] * 2,
        compiler_params=VM,
        name="tables",
    )(hops, pairs)
    at = jnp.where(low, 0, BLK - INNER)
    win = jnp.stack([lax.dynamic_slice_in_dim(x, at, INNER, 0) for x in (mine, other)])
    us, g, gs, acc = pl.pallas_call(
        inner_kernel,
        out_shape=[
            jax.ShapeDtypeStruct((INNER, 6 * COLS, LANES), BF16),
            jax.ShapeDtypeStruct((INNER - 4, 2 * COLS, LANES), F32),
            jax.ShapeDtypeStruct((INNER - 4, 6 * COLS, LANES), BF16),
            jax.ShapeDtypeStruct((8, 2 * COLS, LANES), F32),
        ],
        in_specs=[vmem] * 4,
        out_specs=[vmem] * 4,
        compiler_params=VM,
        name="inner",
    )(win, own, hop_t, pair_t)
    send, img = pl.pallas_call(
        outer_kernel,
        out_shape=[
            jax.ShapeDtypeStruct((72, LANES), F32),
            jax.ShapeDtypeStruct((2, COLS, LANES), F32),
        ],
        in_specs=[vmem] * 9,
        out_specs=[vmem] * 2,
        scratch_shapes=[
            pltpu.VMEM((EDGE, 6 * COLS, LANES), BF16),
            pltpu.VMEM((REACH, 2 * COLS, LANES), F32),
            pltpu.VMEM((EDGE, 6 * COLS, LANES), BF16),
        ],
        compiler_params=VM,
        name="outer",
    )(win, own, recv, hop_t, pair_t, us, g, gs, acc)
    sent = lax.all_gather(send, "eh")
    mom = (sent[0, :3] + sent[1, :3]).reshape(1, 1, 3 * LANES)
    mom = jnp.broadcast_to(mom, (DOMS, 1, 3 * LANES))
    parts = lax.all_to_all(mom, "dom", 0, 0)[:, 0]
    coef = coefficients(parts)[:, :, None]
    coef = jnp.broadcast_to(coef, (4, COLS, LANES))
    return pl.pallas_call(
        combine_kernel,
        out_shape=jax.ShapeDtypeStruct((1, 2, COLS, LANES), F32),
        in_specs=[vmem] * 4,
        out_specs=vmem,
        compiler_params=VM,
        name="combine",
    )(coef, mine, img, sent)


def solution(mesh):
    placed = (
        P("eh", "dom", None, None),
        P("shift", None),
        P("shift", None),
        P(),
        P(),
        P("dom", None),
        P("dom"),
    )
    return jax.shard_map(
        body,
        mesh=mesh,
        in_specs=placed,
        out_specs=P("eh", ("dom", "shift"), None, None),
        check_vma=False,
    )
```
